32 devices in a mesh: parts: 2 (over y), gx: 4 (over z), gy: 4 (over x, core).
Axes of the slice: x: 2, y: 2, z: 4, core: 2. Of those that a mesh axis runs over, the one named last changes fastest.
Arguments:
- tokens: bfloat16 [128, 12288], P(('parts', 'gx'), 'gy'), parts along dimension 0, may hold values from -6 to 6
- w_query: bfloat16 [12288, 12288], P('gy', 'gx'), may hold values from -0.0546875 to 0.0546875
- key_matrix: bfloat16 [12288, 1024], P('gy', 'gx'), may hold values from -0.0546875 to 0.0546875
- value_matrix: bfloat16 [12288, 1024], P('gy', 'gx'), may hold values from -0.0546875 to 0.0546875
- w_output: bfloat16 [12288, 12288], P('gy', 'gx'), may hold values from -0.0546875 to 0.0546875
- stored_keys: bfloat16 [128, 128, 1024], P(('parts', 'gy', 'gx')), parts along dimension 0, may hold values from -260 to 260
- stored_values: bfloat16 [128, 128, 1024], P(('parts', 'gy', 'gx')), parts along dimension 0, may hold values from -6 to 6
- lengths: int32 [128], P(('parts', 'gy', 'gx')), parts along dimension 0, may hold values from 1 to 128, as said below
- positions: int32 [128], P(('parts', 'gy', 'gx')), parts along dimension 0, may hold values from 128 to 4095
Outputs:
- attended: bfloat16 [128, 12288], P(('parts', 'gy'), 'gx'), parts along dimension 0
The draws below stay inside these ranges and needn't reach their ends.
There are 2 independent parts, one for each index of `parts`. The reference program is written for one: setup_inputs(seed, part) draws one part's arguments, and reference() takes and returns one part's arrays. A program takes and returns all parts, laid end to end along the dimension named above; an argument that names none is the same for every part. Nothing has to cross between parts.
Inputs may be any that keep to these rules, and one draw needn't show every extreme that they name: `lengths`: every row has at least one live position, and in every draw some row has all 128.
All inputs are finite; a program needn't handle non-finite values.
Results may differ from the reference program's by a relative error of at most 0.012.
The reference program's roundings to bfloat16 on the way count: a program that leaves them out, or rounds other values in their place, can miss the bound.
Values may be sent and summed in bfloat16 or wider, within the bound.
No kernel may reach another device: no remote copies, remote signals or barrier semaphores. Data moves between devices by JAX's collectives and lax.ppermute only.
A program may use at most 128 MiB of HBM per device.

```python
import jax
import jax.numpy as jnp
from jax import lax

MODEL_WIDTH = 12288
QUERY_HEADS = 96
KEY_VALUE_HEADS = 8
HEAD_WIDTH = 128
DEVICE_ROWS = 4
CONTEXT_LENGTH = 128
TOTAL_ROWS = 64


def draw_lengths(key, part):
    key = jax.random.fold_in(key, 11)
    first_key, second_key = jax.random.split(key)
    drawn = jax.random.randint(first_key, (TOTAL_ROWS,), 1, CONTEXT_LENGTH + 1)
    full_row = jax.random.randint(second_key, (), 0, TOTAL_ROWS)
    return jnp.where(jnp.arange(TOTAL_ROWS) == full_row, CONTEXT_LENGTH, drawn).astype(jnp.int32)


def draw_stored_keys(key, part):
    key = jax.random.fold_in(key, 23)
    base_key = jax.random.fold_in(key, 0)
    array_shape = (TOTAL_ROWS, CONTEXT_LENGTH, KEY_VALUE_HEADS * HEAD_WIDTH)
    base = jnp.clip(jax.random.normal(base_key, array_shape, jnp.float32), -6.0, 6.0)
    return base.astype(jnp.bfloat16)


def touch_ends(entries, rng, smallest, high):
    place = [jax.random.randint(jax.random.fold_in(rng, axis), (), 0, length) for axis, length in enumerate(entries.shape)]
    widest = entries.shape.index(max(entries.shape))
    next_to = place[:widest] + [(place[widest] + 1) % entries.shape[widest]] + place[widest + 1:]
    return entries.at[tuple(place)].set(smallest).at[tuple(next_to)].set(high)


def levels(key, extent, cuts, low, largest):
    factor_of, own = 1.0, jax.random.fold_in(key, 6)
    for axis_at, blocks in cuts:
        steps = jnp.exp(jax.random.uniform(jax.random.fold_in(own, axis_at), (blocks,), jnp.float32, low / len(cuts), largest / len(cuts)))
        factor_of = factor_of * jnp.repeat(steps, extent[axis_at] // blocks).reshape([-1 if axis == axis_at else 1 for axis in range(len(extent))])
    return factor_of


def normal_values(stream_key, shape, scale, bound, cuts=(), held_as=jnp.bfloat16):
    values = jax.random.normal(stream_key, shape, jnp.float32) * scale
    if len(cuts) > 0:
        values = levels(stream_key, shape, cuts, -0.22, 0.18) * values
    return jnp.clip(values, min=-bound, max=bound).astype(held_as)


def setup_inputs(seed: int = 0, part: int = 0) -> dict:
    arg_keys = jax.random.split(jax.random.key(seed), 10)
    part_keys = jax.random.split(jax.random.fold_in(arg_keys[9], part), 10)
    tokens = normal_values(part_keys[0], (TOTAL_ROWS, MODEL_WIDTH), 1.0, 6.0, ((0, 4), (1, 4)))
    w_query = normal_values(arg_keys[1], (MODEL_WIDTH, MODEL_WIDTH), MODEL_WIDTH ** -0.5, 0.0546875, ((0, 4), (1, 4)))
    key_matrix = normal_values(arg_keys[2], (MODEL_WIDTH, KEY_VALUE_HEADS * HEAD_WIDTH), MODEL_WIDTH ** -0.5, 0.0546875, ((0, 4), (1, 4)))
    value_matrix = normal_values(arg_keys[3], (MODEL_WIDTH, KEY_VALUE_HEADS * HEAD_WIDTH), MODEL_WIDTH ** -0.5, 0.0546875, ((0, 4), (1, 4)))
    w_output = normal_values(arg_keys[4], (MODEL_WIDTH, MODEL_WIDTH), MODEL_WIDTH ** -0.5, 0.0546875, ((0, 4), (1, 4)))
    stored_keys = draw_stored_keys(jax.random.fold_in(jax.random.fold_in(arg_keys[9], part), 71), part)
    stored_values = normal_values(part_keys[6], (TOTAL_ROWS, CONTEXT_LENGTH, KEY_VALUE_HEADS * HEAD_WIDTH), 1.0, 6.0, ((0, 16),))
    lengths = draw_lengths(jax.random.fold_in(jax.random.fold_in(arg_keys[9], part), 71), part)
    positions = touch_ends(jax.random.randint(part_keys[8], (TOTAL_ROWS,), CONTEXT_LENGTH, 4096), jax.random.fold_in(part_keys[8], 1), CONTEXT_LENGTH, 4095).astype(jnp.int32)
    return dict(tokens=tokens, w_query=w_query, key_matrix=key_matrix, value_matrix=value_matrix, w_output=w_output, stored_keys=stored_keys, stored_values=stored_values, lengths=lengths, positions=positions)


rope_theta = 1000000.0


def rotary_table(values, positions, heads):
    number_rows = values.shape[0]
    head_size = values.shape[1] // heads
    half_dim = head_size // 2
    wide = values.astype(jnp.float32).reshape(number_rows, heads, head_size)
    frequency = rope_theta ** (-(jnp.arange(half_dim, dtype=jnp.float32) * 2.0) / head_size)
    angles = positions.astype(jnp.float32)[:, None] * frequency[None, :]
    cosine = jnp.cos(angles)[:, None, :]
    sine = jnp.sin(angles)[:, None, :]
    lower_half = wide[..., :half_dim]
    upper_half = wide[..., half_dim:]
    turned = jnp.concatenate([lower_half * cosine - upper_half * sine, upper_half * cosine + lower_half * sine], axis=-1)
    return turned.reshape(values.shape).astype(jnp.bfloat16)


def attend(rotated_query, rotated_key, fresh_value, block_keys, block_values, lengths_block):
    number_rows = rotated_query.shape[0]
    group_size = QUERY_HEADS // KEY_VALUE_HEADS
    logit_scale = 1.0 / (HEAD_WIDTH ** 0.5)
    per_head_queries = rotated_query.astype(jnp.float32).reshape(number_rows, KEY_VALUE_HEADS, group_size, HEAD_WIDTH)
    per_head_keys = block_keys.astype(jnp.float32).reshape(number_rows, CONTEXT_LENGTH, KEY_VALUE_HEADS, HEAD_WIDTH)
    scores = jnp.einsum("rgqd,rpgd->rgqp", per_head_queries, per_head_keys) * logit_scale
    live_mask = (jnp.arange(CONTEXT_LENGTH, dtype=jnp.int32)[None, :] < lengths_block[:, None])[:, None, None, :]
    scores = jnp.where(live_mask, scores, -jnp.inf)
    self_score = jnp.einsum("uojn,uon->uoj", per_head_queries, rotated_key.astype(jnp.float32).reshape(number_rows, KEY_VALUE_HEADS, HEAD_WIDTH)) * logit_scale
    row_max = jnp.maximum(jnp.max(scores, axis=-1), self_score)
    cached_exp = jnp.exp(scores - row_max[..., None])
    own_exp = jnp.exp(self_score - row_max)
    totals = jnp.sum(cached_exp, axis=-1) + own_exp
    weights = (cached_exp / totals[..., None]).astype(jnp.bfloat16)
    self_weight = (own_exp / totals).astype(jnp.bfloat16)
    per_head_values = block_values.astype(jnp.float32).reshape(number_rows, CONTEXT_LENGTH, KEY_VALUE_HEADS, HEAD_WIDTH)
    context_window = jnp.einsum("rgqp,rpgd->rgqd", weights.astype(jnp.float32), per_head_values)
    context_window = context_window + self_weight.astype(jnp.float32)[..., None] * fresh_value.astype(jnp.float32).reshape(number_rows, KEY_VALUE_HEADS, 1, HEAD_WIDTH)
    return context_window.reshape(number_rows, QUERY_HEADS * HEAD_WIDTH).astype(jnp.bfloat16)


def reference(tokens, w_query, key_matrix, value_matrix, w_output, stored_keys, stored_values, lengths, positions):
    query = jnp.dot(tokens, w_query, preferred_element_type=jnp.float32).astype(jnp.bfloat16)
    fresh_key = jnp.dot(tokens, key_matrix, preferred_element_type=jnp.float32).astype(jnp.bfloat16)
    fresh_value = jnp.dot(tokens, value_matrix, preferred_element_type=jnp.float32).astype(jnp.bfloat16)
    rotated_query = rotary_table(query, positions, QUERY_HEADS)
    rotated_key = rotary_table(fresh_key, positions, KEY_VALUE_HEADS)
    block_list = TOTAL_ROWS // DEVICE_ROWS

    def one_block(block):
        return attend(block[0], block[1], block[2], block[3], block[4], block[5])

    pieces = (
        rotated_query.reshape(block_list, DEVICE_ROWS, QUERY_HEADS * HEAD_WIDTH),
        rotated_key.reshape(block_list, DEVICE_ROWS, KEY_VALUE_HEADS * HEAD_WIDTH),
        fresh_value.reshape(block_list, DEVICE_ROWS, KEY_VALUE_HEADS * HEAD_WIDTH),
        stored_keys.reshape(block_list, DEVICE_ROWS, CONTEXT_LENGTH, KEY_VALUE_HEADS * HEAD_WIDTH),
        stored_values.reshape(block_list, DEVICE_ROWS, CONTEXT_LENGTH, KEY_VALUE_HEADS * HEAD_WIDTH),
        lengths.reshape(block_list, DEVICE_ROWS),
    )
    context_window = lax.map(one_block, pieces).reshape(TOTAL_ROWS, QUERY_HEADS * HEAD_WIDTH)
    return jnp.dot(context_window, w_output, preferred_element_type=jnp.float32).astype(jnp.bfloat16)
```

```python
import functools

import jax
import jax.numpy as jnp
from jax import lax
from jax.experimental import pallas as pl
from jax.experimental.pallas import tpu as pltpu
from jax.sharding import PartitionSpec as P

QUERY_HEADS = 96
KEY_VALUE_HEADS = 8
HEAD_WIDTH = 128
CONTEXT_LENGTH = 128
GROUP = QUERY_HEADS // KEY_VALUE_HEADS


rope_theta = 1000000.0

VMEM = pl.BlockSpec(memory_space=pltpu.VMEM)
SMEM = pl.BlockSpec(memory_space=pltpu.SMEM)


def rotary_angles(positions):
    half_dim = HEAD_WIDTH // 2
    frequency = rope_theta ** (-(jnp.arange(half_dim, dtype=jnp.float32) * 2.0) / HEAD_WIDTH)
    return positions.astype(jnp.float32)[:, None] * frequency[None, :]


def rotary_table(values, positions, heads):
    number_rows = values.shape[0]
    head_size = values.shape[1] // heads
    half_dim = head_size // 2
    wide = values.astype(jnp.float32).reshape(number_rows, heads, head_size)
    angles = rotary_angles(positions)
    cosine = jnp.cos(angles)[:, None, :]
    sine = jnp.sin(angles)[:, None, :]
    lower_half = wide[..., :half_dim]
    upper_half = wide[..., half_dim:]
    turned = jnp.concatenate(
        [lower_half * cosine - upper_half * sine, upper_half * cosine + lower_half * sine], axis=-1
    )
    return turned.reshape(values.shape).astype(jnp.bfloat16)


def attend(rotated_query, rotated_key, fresh_value, device_keys, device_values, lengths):
    number_rows = rotated_query.shape[0]
    logit_scale = 1.0 / HEAD_WIDTH**0.5
    per_head_queries = rotated_query.reshape(number_rows, KEY_VALUE_HEADS, GROUP, HEAD_WIDTH)
    per_head_keys = device_keys.reshape(number_rows, CONTEXT_LENGTH, KEY_VALUE_HEADS, HEAD_WIDTH)
    scores = (
        jnp.einsum(
            "rgqd,rpgd->rgqp", per_head_queries, per_head_keys, preferred_element_type=jnp.float32
        )
        * logit_scale
    )
    live_mask = (jnp.arange(CONTEXT_LENGTH, dtype=jnp.int32)[None, :] < lengths[:, None])[
        :, None, None, :
    ]
    scores = jnp.where(live_mask, scores, -jnp.inf)
    self_score = (
        jnp.einsum(
            "uojn,uon->uoj",
            per_head_queries,
            rotated_key.reshape(number_rows, KEY_VALUE_HEADS, HEAD_WIDTH),
            preferred_element_type=jnp.float32,
        )
        * logit_scale
    )
    row_max = jnp.maximum(jnp.max(scores, axis=-1), self_score)
    cached_exp = jnp.exp(scores - row_max[..., None])
    own_exp = jnp.exp(self_score - row_max)
    totals = jnp.sum(cached_exp, axis=-1) + own_exp
    weights = (cached_exp / totals[..., None]).astype(jnp.bfloat16)
    self_weight = (own_exp / totals).astype(jnp.bfloat16)
    per_head_values = device_values.reshape(
        number_rows, CONTEXT_LENGTH, KEY_VALUE_HEADS, HEAD_WIDTH
    )
    context_window = jnp.einsum(
        "rgqp,rpgd->rgqd", weights, per_head_values, preferred_element_type=jnp.float32
    )
    context_window = context_window + self_weight.astype(jnp.float32)[
        ..., None
    ] * fresh_value.astype(jnp.float32).reshape(number_rows, KEY_VALUE_HEADS, 1, HEAD_WIDTH)
    return context_window.reshape(number_rows, QUERY_HEADS * HEAD_WIDTH).astype(jnp.bfloat16)


def general_shards(
    tokens,
    w_query,
    key_matrix,
    value_matrix,
    w_output,
    stored_keys,
    stored_values,
    lengths,
    positions,
):
    q_width = w_query.shape[1]
    kv_width = key_matrix.shape[1]
    piece = lax.all_gather(tokens, "gx", axis=0, tiled=True)
    partials = jnp.concatenate(
        [
            jnp.dot(piece, w_query, preferred_element_type=jnp.float32),
            jnp.dot(piece, key_matrix, preferred_element_type=jnp.float32),
            jnp.dot(piece, value_matrix, preferred_element_type=jnp.float32),
        ],
        axis=1,
    )
    summed = lax.psum_scatter(partials, "gy", scatter_dimension=0, tiled=True)
    query = summed[:, :q_width].astype(jnp.bfloat16)
    fresh_key = summed[:, q_width : q_width + kv_width].astype(jnp.bfloat16)
    fresh_value = summed[:, q_width + kv_width :].astype(jnp.bfloat16)
    query_rows, key_row_matrix, value_rows = (
        lax.all_to_all(query, "gx", split_axis=0, concat_axis=1, tiled=True),
        lax.all_to_all(fresh_key, "gx", split_axis=0, concat_axis=1, tiled=True),
        lax.all_to_all(fresh_value, "gx", split_axis=0, concat_axis=1, tiled=True),
    )
    rotated_query = rotary_table(query_rows, positions, QUERY_HEADS)
    rotated_key = rotary_table(key_row_matrix, positions, KEY_VALUE_HEADS)
    context_window = attend(
        rotated_query, rotated_key, value_rows, stored_keys, stored_values, lengths
    )
    out_width = w_output.shape[1]
    block_list = lax.all_to_all(context_window[None], "gy", split_axis=2, concat_axis=0, tiled=True)
    products = jnp.einsum(
        "jrd,de->jre",
        lax.all_gather(block_list, "gx", axis=1, tiled=True),
        w_output,
        preferred_element_type=jnp.float32,
    )
    products = products.reshape(-1, out_width)
    result = lax.psum_scatter(products, "gy", scatter_dimension=0, tiled=True)
    return result.astype(jnp.bfloat16)


SIDE = 4
ROWS = 4
BLOCK = SIDE * ROWS
SLOTS = 16
OWNERS = (0, 2, 1, 3)


def call(body, outs, args, specs, scratch=(), limit=8, flops=0, moved=0):
    return pl.pallas_call(
        body,
        out_shape=outs,
        in_specs=specs,
        out_specs=jax.tree.map(lambda _: VMEM, outs),
        scratch_shapes=list(scratch),
        compiler_params=pltpu.CompilerParams(vmem_limit_bytes=limit << 20),
        cost_estimate=pl.CostEstimate(flops=flops, bytes_accessed=moved, transcendentals=0),
    )(*args)


def partners(block, axis, distances=(3, 2, 1)):
    got = {
        k: lax.ppermute(block(k), axis, [(p, p ^ k) for p in range(SIDE)]) for k in distances
    }
    return [got[k] for k in (1, 2, 3)]


def project_body(tile, x0, x1, x2, x3, wq, wk, wv, keep, send, rows):
    m = lax.axis_index("gx") ^ lax.axis_index("gy")
    for s, x in enumerate((x0, x1, x2, x3)):
        d = s ^ m
        place = ((d & 1) << 1) | (d >> 1)
        rows[pl.ds(pl.multiple_of(place * BLOCK, BLOCK), BLOCK), :] = x[...]

    def put(w, c, width, head):
        acc = jnp.dot(rows[...], w[:, pl.ds(c, width)], preferred_element_type=jnp.float32)
        for k in range(width // HEAD_WIDTH):
            at = pl.ds(pl.multiple_of((head + k) * BLOCK, BLOCK), BLOCK)
            part = acc[:, k * HEAD_WIDTH : (k + 1) * HEAD_WIDTH]
            for b in range(2):
                keep[b, at, :] = part[b * BLOCK : (b + 1) * BLOCK]
                send[b, at, :] = part[(2 + b) * BLOCK : (3 + b) * BLOCK]

    per = tile // HEAD_WIDTH

    def step(n, _):
        put(wq, pl.multiple_of(n * tile, tile), tile, n * per)
        return 0

    lax.fori_loop(0, wq.shape[1] // tile, step, 0)
    qh, kh = wq.shape[1] // HEAD_WIDTH, wk.shape[1] // HEAD_WIDTH
    put(wk, 0, wk.shape[1], qh)
    put(wv, 0, wv.shape[1], qh + kh)


def spread_body(groups, keep, got, across, out0, out1, out2, out3, slots):
    j = lax.axis_index("gx")
    qh = groups * GROUP
    for g in range(groups):
        for u in range(SLOTS):
            if u < GROUP:
                h = g * GROUP + u
            elif u == GROUP:
                h = qh + g
            elif u == GROUP + 1:
                h = qh + groups + g
            else:
                h = None
            at = (g * SLOTS + u) * BLOCK
            if h is None:
                slots[at : at + BLOCK, :] = jnp.zeros((BLOCK, HEAD_WIDTH), jnp.float32)
            else:
                src = slice(h * BLOCK, (h + 1) * BLOCK)
                total = (keep[0, src, :] + got[0, src, :]) + across[src, :]
                slots[at : at + BLOCK, :] = total.astype(jnp.bfloat16).astype(jnp.float32)
    wide = groups * SLOTS
    for e, out in enumerate((out0, out1, out2, out3)):
        for t in range(ROWS):
            row = (j ^ e) * ROWS + t
            out[t * wide : (t + 1) * wide, :] = slots[pl.ds(row, wide, stride=BLOCK), :].astype(
                jnp.bfloat16
            )


def attend_body(
    groups, lengths, a0, a1, a2, a3, cosine, sine, keys, values, c0, c1, c2, c3, held
):
    i, j = lax.axis_index("gy"), lax.axis_index("gx")
    scale = 1.0 / HEAD_WIDTH**0.5
    for e, a in enumerate((a0, a1, a2, a3)):
        held[e] = a[...]
    wide = groups * SLOTS
    slot = lax.broadcasted_iota(jnp.int32, (wide, HEAD_WIDTH), 0) % SLOTS
    is_value = slot == GROUP + 1
    spot = lax.broadcasted_iota(jnp.int32, (SLOTS, CONTEXT_LENGTH), 1)
    for f, c in enumerate((c0, c1, c2, c3)):
        source = i ^ f
        block = held.at[source ^ j]
        for t in range(ROWS):
            raw = block[t * wide : (t + 1) * wide, :].astype(jnp.float32)
            turned = (
                raw * cosine[t : t + 1, :]
                + pltpu.roll(raw, HEAD_WIDTH // 2, 1) * sine[t : t + 1, :]
            )
            turned = jnp.where(is_value, raw, turned).astype(jnp.bfloat16)
            live = spot < lengths[t]
            for g in range(groups):
                at = pl.ds(pl.multiple_of((source * groups + g) * HEAD_WIDTH, HEAD_WIDTH), HEAD_WIDTH)
                q = turned[g * SLOTS : (g + 1) * SLOTS]
                wide_q = q.astype(jnp.float32)
                own_key = wide_q[GROUP : GROUP + 1]
                own_value = wide_q[GROUP + 1 : GROUP + 2]
                scores = lax.dot_general(
                    q, keys[t, :, at], (((1,), (1,)), ((), ())), preferred_element_type=jnp.float32
                )
                scores = jnp.where(live, scores * scale, -jnp.inf)
                own = jnp.sum(wide_q * own_key, axis=1, keepdims=True) * scale
                top = jnp.maximum(jnp.max(scores, axis=1, keepdims=True), own)
                cached = jnp.exp(scores - top)
                own = jnp.exp(own - top)
                total = jnp.sum(cached, axis=1, keepdims=True) + own
                weights = (cached / total).astype(jnp.bfloat16)
                own = (own / total).astype(jnp.bfloat16).astype(jnp.float32)
                context = jnp.dot(weights, values[t, :, at], preferred_element_type=jnp.float32)
                context = context + own * own_value
                first = t * wide + g * SLOTS
                c[first : first + SLOTS, :] = context.astype(jnp.bfloat16)


def turn_body(groups, c0, c1, c2, c3, out, slots):
    i = lax.axis_index("gy")
    wide = groups * SLOTS
    size = ROWS * wide
    for f, c in enumerate((c0, c1, c2, c3)):
        slots[pl.ds(pl.multiple_of((i ^ f) * size, size), size), :] = c[...].astype(jnp.float32)
    for g in range(groups):
        for u in range(GROUP):
            h = g * GROUP + u
            out[:, h * HEAD_WIDTH : (h + 1) * HEAD_WIDTH] = slots[
                pl.ds(g * SLOTS + u, BLOCK, stride=wide), :
            ].astype(jnp.bfloat16)


def output_body(tile, x0, x1, x2, x3, w, keep, send, rows, ordered):
    i, j = lax.axis_index("gy"), lax.axis_index("gx")
    for s, x in enumerate((x0, x1, x2, x3)):
        rows[pl.ds(pl.multiple_of((j ^ s) * BLOCK, BLOCK), BLOCK), :] = x[...]
    count = SIDE * BLOCK
    r = lax.broadcasted_iota(jnp.int32, (count, count), 0)
    c = lax.broadcasted_iota(jnp.int32, (count, count), 1)
    place = r >> 4
    owner = i ^ (((place & 1) << 1) | (place >> 1))
    wanted = ((r & 12) << 2) | (owner << 2) | (r & 3)
    swap = jnp.where(c == wanted, 1.0, 0.0).astype(jnp.bfloat16)
    ordered[...] = jnp.dot(swap, rows[...], preferred_element_type=jnp.float32).astype(
        jnp.bfloat16
    )

    def step(n, _):
        at = pl.ds(pl.multiple_of(n * tile, tile), tile)
        acc = jnp.dot(ordered[...], w[:, at], preferred_element_type=jnp.float32)
        keep[:, at] = acc[: 2 * BLOCK]
        send[:, at] = acc[2 * BLOCK :]
        return 0

    lax.fori_loop(0, w.shape[1] // tile, step, 0)


def square_shards(
    tokens,
    w_query,
    key_matrix,
    value_matrix,
    w_output,
    stored_keys,
    stored_values,
    lengths,
    positions,
):
    f32, bf16 = jnp.float32, jnp.bfloat16
    depth, q_width = w_query.shape
    kv_width = key_matrix.shape[1]
    groups = kv_width // HEAD_WIDTH
    heads = (q_width + 2 * kv_width) // HEAD_WIDTH
    wide = groups * SLOTS

    angles = rotary_angles(positions)
    cosine, sine = jnp.cos(angles), jnp.sin(angles)
    cosine = jnp.concatenate([cosine, cosine], axis=1)
    sine = jnp.concatenate([-sine, sine], axis=1)

    near = partners(lambda k: tokens, "gx")
    half = jax.ShapeDtypeStruct((2, heads * BLOCK, HEAD_WIDTH), f32)
    tile = 512
    keep, send = call(
        functools.partial(project_body, tile),
        [half, half],
        (tokens, *near, w_query, key_matrix, value_matrix),
        [VMEM] * 7,
        [pltpu.VMEM((SIDE * BLOCK, depth), bf16)],
        flops=2 * SIDE * BLOCK * depth * heads * HEAD_WIDTH,
        moved=2 * depth * heads * HEAD_WIDTH,
    )
    got = lax.ppermute(send, "gy", [(p, p ^ 1) for p in range(SIDE)])
    across = lax.ppermute(keep[1] + got[1], "gy", [(p, p ^ 2) for p in range(SIDE)])
    piece = jax.ShapeDtypeStruct((ROWS * wide, HEAD_WIDTH), bf16)
    mine = call(
        functools.partial(spread_body, groups),
        [piece] * SIDE,
        (keep, got, across),
        [VMEM] * 3,
        [pltpu.VMEM((wide * BLOCK, HEAD_WIDTH), f32)],
    )
    others = partners(lambda k: mine[k], "gx")
    context = call(
        functools.partial(attend_body, groups),
        [piece] * SIDE,
        (lengths, mine[0], *others, cosine, sine, stored_keys, stored_values),
        [SMEM] + [VMEM] * 8,
        [pltpu.VMEM((SIDE, ROWS * wide, HEAD_WIDTH), bf16)],
    )
    others = partners(lambda k: context[k], "gy", (2, 3, 1))
    rows = call(
        functools.partial(turn_body, groups),
        jax.ShapeDtypeStruct((BLOCK, groups * GROUP * HEAD_WIDTH), bf16),
        (context[0], *others),
        [VMEM] * 4,
        [pltpu.VMEM((SIDE * ROWS * wide, HEAD_WIDTH), f32)],
    )
    near = partners(lambda k: rows, "gx")
    depth, out_width = w_output.shape
    half = jax.ShapeDtypeStruct((2 * BLOCK, out_width), f32)
    keep, send = call(
        functools.partial(output_body, tile),
        [half, half],
        (rows, *near, w_output),
        [VMEM] * 5,
        [pltpu.VMEM((SIDE * BLOCK, depth), bf16)] * 2,
        flops=2 * SIDE * BLOCK * depth * out_width,
        moved=2 * depth * out_width,
    )
    got = lax.ppermute(send, "gy", [(p, p ^ 1) for p in range(SIDE)])
    across = lax.ppermute(
        keep[BLOCK:] + got[BLOCK:], "gy", [(p, p ^ 2) for p in range(SIDE)]
    )
    return ((keep[:BLOCK] + got[:BLOCK]) + across).astype(bf16)


def shards(*args):
    tokens, w_query, key_matrix, _, w_output, stored_keys, _, lengths, _ = args
    whole_heads = w_query.shape[1] % (GROUP * HEAD_WIDTH) == 0
    groups = key_matrix.shape[1] // HEAD_WIDTH
    square = (
        lax.axis_size("gx") == SIDE
        and lax.axis_size("gy") == SIDE
        and lengths.shape[0] == ROWS
        and tokens.shape[0] == BLOCK
        and whole_heads
        and groups * HEAD_WIDTH == key_matrix.shape[1]
        and groups * GROUP * HEAD_WIDTH == w_query.shape[1] == w_output.shape[0]
        and w_output.shape[1] % 512 == 0
        and w_query.shape[1] % 512 == 0
    )
    return square_shards(*args) if square else general_shards(*args)


def solution(mesh):
    in_specs = (
        P(("parts", "gx"), "gy"),
        P("gy", "gx"),
        P("gy", "gx"),
        P("gy", "gx"),
        P("gy", "gx"),
        P(("parts", "gy", "gx"), None, None),
        P(("parts", "gy", "gx"), None, None),
        P(("parts", "gy", "gx")),
        P(("parts", "gy", "gx")),
    )
    out_specs = P(("parts", "gy"), "gx")
    return jax.shard_map(shards, mesh=mesh, in_specs=in_specs, out_specs=out_specs, check_vma=False)
```

```python
import functools
import math

import jax
import jax.numpy as jnp
from jax import lax
from jax.experimental import pallas as pl
from jax.experimental.pallas import tpu as pltpu
from jax.sharding import PartitionSpec as P

QUERY_HEADS = 96
KEY_VALUE_HEADS = 8
HEAD_WIDTH = 128
CONTEXT_LENGTH = 128
GROUP = QUERY_HEADS // KEY_VALUE_HEADS


rope_theta = 1000000.0

VMEM = pl.BlockSpec(memory_space=pltpu.VMEM)
SMEM = pl.BlockSpec(memory_space=pltpu.SMEM)


def rotary_angles(positions):
    half_dim = HEAD_WIDTH // 2
    frequency = rope_theta ** (-(jnp.arange(half_dim, dtype=jnp.float32) * 2.0) / HEAD_WIDTH)
    return positions.astype(jnp.float32)[:, None] * frequency[None, :]


def rotary_table(values, positions, heads):
    number_rows = values.shape[0]
    head_size = values.shape[1] // heads
    half_dim = head_size // 2
    wide = values.astype(jnp.float32).reshape(number_rows, heads, head_size)
    angles = rotary_angles(positions)
    cosine = jnp.cos(angles)[:, None, :]
    sine = jnp.sin(angles)[:, None, :]
    lower_half = wide[..., :half_dim]
    upper_half = wide[..., half_dim:]
    turned = jnp.concatenate(
        [lower_half * cosine - upper_half * sine, upper_half * cosine + lower_half * sine], axis=-1
    )
    return turned.reshape(values.shape).astype(jnp.bfloat16)


def attend(rotated_query, rotated_key, fresh_value, device_keys, device_values, lengths):
    number_rows = rotated_query.shape[0]
    logit_scale = 1.0 / HEAD_WIDTH**0.5
    per_head_queries = rotated_query.reshape(number_rows, KEY_VALUE_HEADS, GROUP, HEAD_WIDTH)
    per_head_keys = device_keys.reshape(number_rows, CONTEXT_LENGTH, KEY_VALUE_HEADS, HEAD_WIDTH)
    scores = (
        jnp.einsum(
            "rgqd,rpgd->rgqp", per_head_queries, per_head_keys, preferred_element_type=jnp.float32
        )
        * logit_scale
    )
    live_mask = (jnp.arange(CONTEXT_LENGTH, dtype=jnp.int32)[None, :] < lengths[:, None])[
        :, None, None, :
    ]
    scores = jnp.where(live_mask, scores, -jnp.inf)
    self_score = (
        jnp.einsum(
            "uojn,uon->uoj",
            per_head_queries,
            rotated_key.reshape(number_rows, KEY_VALUE_HEADS, HEAD_WIDTH),
            preferred_element_type=jnp.float32,
        )
        * logit_scale
    )
    row_max = jnp.maximum(jnp.max(scores, axis=-1), self_score)
    cached_exp = jnp.exp(scores - row_max[..., None])
    own_exp = jnp.exp(self_score - row_max)
    totals = jnp.sum(cached_exp, axis=-1) + own_exp
    weights = (cached_exp / totals[..., None]).astype(jnp.bfloat16)
    self_weight = (own_exp / totals).astype(jnp.bfloat16)
    per_head_values = device_values.reshape(
        number_rows, CONTEXT_LENGTH, KEY_VALUE_HEADS, HEAD_WIDTH
    )
    context_window = jnp.einsum(
        "rgqp,rpgd->rgqd", weights, per_head_values, preferred_element_type=jnp.float32
    )
    context_window = context_window + self_weight.astype(jnp.float32)[
        ..., None
    ] * fresh_value.astype(jnp.float32).reshape(number_rows, KEY_VALUE_HEADS, 1, HEAD_WIDTH)
    return context_window.reshape(number_rows, QUERY_HEADS * HEAD_WIDTH).astype(jnp.bfloat16)


def general_shards(
    tokens,
    w_query,
    key_matrix,
    value_matrix,
    w_output,
    stored_keys,
    stored_values,
    lengths,
    positions,
):
    q_width = w_query.shape[1]
    kv_width = key_matrix.shape[1]
    piece = lax.all_gather(tokens, "gx", axis=0, tiled=True)
    partials = jnp.concatenate(
        [
            jnp.dot(piece, w_query, preferred_element_type=jnp.float32),
            jnp.dot(piece, key_matrix, preferred_element_type=jnp.float32),
            jnp.dot(piece, value_matrix, preferred_element_type=jnp.float32),
        ],
        axis=1,
    )
    summed = lax.psum_scatter(partials, "gy", scatter_dimension=0, tiled=True)
    query = summed[:, :q_width].astype(jnp.bfloat16)
    fresh_key = summed[:, q_width : q_width + kv_width].astype(jnp.bfloat16)
    fresh_value = summed[:, q_width + kv_width :].astype(jnp.bfloat16)
    query_rows, key_row_matrix, value_rows = (
        lax.all_to_all(query, "gx", split_axis=0, concat_axis=1, tiled=True),
        lax.all_to_all(fresh_key, "gx", split_axis=0, concat_axis=1, tiled=True),
        lax.all_to_all(fresh_value, "gx", split_axis=0, concat_axis=1, tiled=True),
    )
    rotated_query = rotary_table(query_rows, positions, QUERY_HEADS)
    rotated_key = rotary_table(key_row_matrix, positions, KEY_VALUE_HEADS)
    context_window = attend(
        rotated_query, rotated_key, value_rows, stored_keys, stored_values, lengths
    )
    out_width = w_output.shape[1]
    block_list = lax.all_to_all(context_window[None], "gy", split_axis=2, concat_axis=0, tiled=True)
    products = jnp.einsum(
        "jrd,de->jre",
        lax.all_gather(block_list, "gx", axis=1, tiled=True),
        w_output,
        preferred_element_type=jnp.float32,
    )
    products = products.reshape(-1, out_width)
    result = lax.psum_scatter(products, "gy", scatter_dimension=0, tiled=True)
    return result.astype(jnp.bfloat16)


SIDE = 4
ROWS = 4
BLOCK = SIDE * ROWS
SLOTS = 16
FROM = (0, 3, 1, 2)


def call(body, outs, args, specs, scratch=(), limit=8, flops=0, moved=0):
    return pl.pallas_call(
        body,
        out_shape=outs,
        in_specs=specs,
        out_specs=jax.tree.map(lambda _: VMEM, outs),
        scratch_shapes=list(scratch),
        compiler_params=pltpu.CompilerParams(vmem_limit_bytes=limit << 20),
        cost_estimate=pl.CostEstimate(flops=flops, bytes_accessed=moved, transcendentals=0),
    )(*args)


def fetch_body(parts, *refs):
    sems, done = refs[-1], refs[-2]
    targets = refs[-2 - len(parts) : -2]
    copies = []
    for n, (source, index, pieces) in enumerate(parts):
        size = refs[source].shape[0] // pieces
        for k in range(pieces):
            at = pl.ds(k * size, size)
            copies.append(
                pltpu.make_async_copy(
                    refs[source].at[(at, *index)], targets[n].at[at], sems.at[len(copies)]
                )
            )
    for copy in copies:
        copy.start()
    done[...] = jnp.zeros_like(done)
    for copy in copies:
        copy.wait()


def fetch(parts, *after):
    sources, plan, outs = [], [], []
    for array, *columns in parts:
        if not any(array is s for s in sources):
            sources.append(array)
        at = next(n for n, s in enumerate(sources) if s is array)
        index = (slice(None), pl.ds(*columns)) if columns else ()
        shape = (array.shape[0], columns[1]) if columns else array.shape
        plan.append((at, index[1:], 4))
        outs.append(pltpu.VMEM(shape, array.dtype))
    moved = 2 * sum(math.prod(out.shape) for out in outs)
    done = jax.ShapeDtypeStruct((8, HEAD_WIDTH), jnp.float32)
    return pl.pallas_call(
        functools.partial(fetch_body, plan),
        out_shape=[*outs, done],
        in_specs=[pl.BlockSpec(memory_space=pltpu.HBM)] * len(sources) + [VMEM] * len(after),
        out_specs=[VMEM] * (len(outs) + 1),
        scratch_shapes=[pltpu.SemaphoreType.DMA((4 * len(outs),))],
        compiler_params=pltpu.CompilerParams(vmem_limit_bytes=36 << 20),
        cost_estimate=pl.CostEstimate(flops=0, bytes_accessed=moved, transcendentals=0),
    )(*sources, *after)


def partners(block, axis):
    return [lax.ppermute(block(k), axis, [(p, p ^ k) for p in range(SIDE)]) for k in FROM[1:]]


def project_body(tile, count, x0, x1, x2, x3, *refs):
    weights = refs[:count]
    keep, send, rows = refs[count:]
    m = lax.axis_index("gx") ^ lax.axis_index("gy")
    for s, x in zip(FROM, (x0, x1, x2, x3)):
        d = s ^ m
        place = ((d & 1) << 1) | (d >> 1)
        rows[pl.ds(pl.multiple_of(place * BLOCK, BLOCK), BLOCK), :] = x[...]

    def put(w, c, width, head):
        acc = jnp.dot(rows[...], w[:, pl.ds(c, width)], preferred_element_type=jnp.float32)
        for k in range(width // HEAD_WIDTH):
            at = pl.ds(pl.multiple_of((head + k) * BLOCK, BLOCK), BLOCK)
            part = acc[:, k * HEAD_WIDTH : (k + 1) * HEAD_WIDTH]
            for b in range(2):
                keep[b, at, :] = part[b * BLOCK : (b + 1) * BLOCK]
                send[b, at, :] = part[(2 + b) * BLOCK : (3 + b) * BLOCK]

    head = 0
    for w in weights:
        width = min(tile, w.shape[1])
        per = width // HEAD_WIDTH

        def step(n, _):
            put(w, pl.multiple_of(n * width, width), width, head + n * per)
            return 0

        lax.fori_loop(0, w.shape[1] // width, step, 0)
        head += w.shape[1] // HEAD_WIDTH


def spread_body(groups, keep0, got0, across0, keep1, got1, across1, ready, *refs):
    outs, slots = refs[:-1], refs[-1]
    j = lax.axis_index("gx")
    first = keep0.shape[1] // BLOCK
    qh = groups * GROUP
    for g in range(groups):
        for u in range(SLOTS):
            if u < GROUP:
                h = g * GROUP + u
            elif u == GROUP:
                h = qh + g
            elif u == GROUP + 1:
                h = qh + groups + g
            else:
                h = None
            at = (g * SLOTS + u) * BLOCK
            if h is None:
                slots[at : at + BLOCK, :] = jnp.zeros((BLOCK, HEAD_WIDTH), jnp.float32)
                continue
            keep, got, across = (keep0, got0, across0) if h < first else (keep1, got1, across1)
            h = h if h < first else h - first
            src = slice(h * BLOCK, (h + 1) * BLOCK)
            total = (keep[0, src, :] + got[0, src, :]) + across[src, :]
            slots[at : at + BLOCK, :] = total.astype(jnp.bfloat16).astype(jnp.float32)
    wide = groups * SLOTS
    for e, out in enumerate(outs):
        for t in range(ROWS):
            row = (j ^ e) * ROWS + t
            out[t * wide : (t + 1) * wide, :] = slots[pl.ds(row, wide, stride=BLOCK), :].astype(
                jnp.bfloat16
            )


def attend_body(
    groups, lengths, a0, a1, a2, a3, cosine, sine, keys, values, c0, c1, c2, c3, held
):
    j = lax.axis_index("gx")
    m = j ^ lax.axis_index("gy")
    scale = 1.0 / HEAD_WIDTH**0.5
    wide = groups * SLOTS
    span = groups * HEAD_WIDTH
    slot = lax.broadcasted_iota(jnp.int32, (wide, HEAD_WIDTH), 0)
    is_value = slot % SLOTS == GROUP + 1
    of_group = [slot // SLOTS == g for g in range(groups)]
    spot = lax.broadcasted_iota(jnp.int32, (wide, CONTEXT_LENGTH), 1)
    pieces = [(e, t) for e in range(SIDE) for t in range(ROWS)]
    heads = dict(zip(FROM, (a0, a1, a2, a3)))

    def lanes(e):
        return pl.ds(pl.multiple_of((j ^ e) * span, span), span)

    def each_group(block, row):
        out = block[row : row + 1]
        for g in range(1, groups):
            at = g * SLOTS + row
            out = jnp.where(of_group[g], block[at : at + 1], out)
        return out

    scores, owns, fresh = [], [], []
    for e, t in pieces:
        raw = heads[e][t * wide : (t + 1) * wide, :].astype(jnp.float32)
        turned = (
            raw * cosine[t : t + 1, :] + pltpu.roll(raw, HEAD_WIDTH // 2, 1) * sine[t : t + 1, :]
        )
        q = jnp.where(is_value, raw, turned).astype(jnp.bfloat16)
        wide_q = q.astype(jnp.float32)
        spread = jnp.concatenate(
            [jnp.where(of_group[g], wide_q, 0.0) for g in range(groups)], axis=1
        ).astype(jnp.bfloat16)
        found = lax.dot_general(
            spread,
            keys[t, :, lanes(e)],
            (((1,), (1,)), ((), ())),
            preferred_element_type=jnp.float32,
        )
        scores.append(jnp.where(spot < lengths[t], found * scale, -jnp.inf))
        owns.append(
            jnp.sum(wide_q * each_group(wide_q, GROUP), axis=1, keepdims=True) * scale
        )
        fresh.append(each_group(wide_q, GROUP + 1))
    tops = [
        jnp.maximum(jnp.max(s, axis=1, keepdims=True), own) for s, own in zip(scores, owns)
    ]
    cached = [jnp.exp(s - top) for s, top in zip(scores, tops)]
    owns = [jnp.exp(own - top) for own, top in zip(owns, tops)]
    totals = [jnp.sum(w, axis=1, keepdims=True) + own for w, own in zip(cached, owns)]
    weights = [(w / total).astype(jnp.bfloat16) for w, total in zip(cached, totals)]
    owns = [
        (own / total).astype(jnp.bfloat16).astype(jnp.float32) for own, total in zip(owns, totals)
    ]
    for n, (e, t) in enumerate(pieces):
        found = jnp.dot(weights[n], values[t, :, lanes(e)], preferred_element_type=jnp.float32)
        context = found[:, :HEAD_WIDTH]
        for g in range(1, groups):
            context = jnp.where(
                of_group[g], found[:, g * HEAD_WIDTH : (g + 1) * HEAD_WIDTH], context
            )
        context = context + owns[n] * fresh[n]
        held[e ^ m, t * wide : (t + 1) * wide, :] = context.astype(jnp.bfloat16)
    for f, c in enumerate((c0, c1, c2, c3)):
        c[...] = held[f]


def turn_body(groups, c0, c1, c2, c3, out, slots):
    i = lax.axis_index("gy")
    wide = groups * SLOTS
    size = ROWS * wide
    for f, c in zip(FROM, (c0, c1, c2, c3)):
        slots[pl.ds(pl.multiple_of((i ^ f) * size, size), size), :] = c[...].astype(jnp.float32)
    for g in range(groups):
        for u in range(GROUP):
            h = g * GROUP + u
            out[:, h * HEAD_WIDTH : (h + 1) * HEAD_WIDTH] = slots[
                pl.ds(g * SLOTS + u, BLOCK, stride=wide), :
            ].astype(jnp.bfloat16)


def output_body(tile, x0, x1, x2, x3, w0, w1, keep, send, rows, ordered):
    i, j = lax.axis_index("gy"), lax.axis_index("gx")
    for s, x in zip(FROM, (x0, x1, x2, x3)):
        rows[pl.ds(pl.multiple_of((j ^ s) * BLOCK, BLOCK), BLOCK), :] = x[...]
    count = SIDE * BLOCK
    r = lax.broadcasted_iota(jnp.int32, (count, count), 0)
    c = lax.broadcasted_iota(jnp.int32, (count, count), 1)
    place = r >> 4
    owner = i ^ (((place & 1) << 1) | (place >> 1))
    wanted = ((r & 12) << 2) | (owner << 2) | (r & 3)
    swap = jnp.where(c == wanted, 1.0, 0.0).astype(jnp.bfloat16)
    ordered[...] = jnp.dot(swap, rows[...], preferred_element_type=jnp.float32).astype(
        jnp.bfloat16
    )

    for w, first in ((w0, 0), (w1, w0.shape[1])):

        def step(n, _):
            c = pl.multiple_of(n * tile, tile)
            acc = jnp.dot(ordered[...], w[:, pl.ds(c, tile)], preferred_element_type=jnp.float32)
            at = pl.ds(pl.multiple_of(first + n * tile, tile), tile)
            keep[:, at] = acc[: 2 * BLOCK]
            send[:, at] = acc[2 * BLOCK :]
            return 0

        lax.fori_loop(0, w.shape[1] // tile, step, 0)


def square_shards(
    tokens,
    w_query,
    key_matrix,
    value_matrix,
    w_output,
    stored_keys,
    stored_values,
    lengths,
    positions,
):
    f32, bf16 = jnp.float32, jnp.bfloat16
    depth, q_width = w_query.shape
    kv_width = key_matrix.shape[1]
    groups = kv_width // HEAD_WIDTH
    wide = groups * SLOTS

    angles = rotary_angles(positions)
    cosine, sine = jnp.cos(angles), jnp.sin(angles)
    cosine = jnp.concatenate([cosine, cosine], axis=1)
    sine = jnp.concatenate([-sine, sine], axis=1)

    near = partners(lambda k: tokens, "gx")
    tile = 512
    part = q_width // 2
    w_first, w_second, key_matrix, value_matrix, _ = fetch(
        [(w_query, 0, part), (w_query, part, part), (key_matrix,), (value_matrix,)]
    )
    sums = []
    for weights in ((w_first,), (w_second, key_matrix, value_matrix)):
        columns = sum(w.shape[1] for w in weights)
        half = jax.ShapeDtypeStruct((2, columns // HEAD_WIDTH * BLOCK, HEAD_WIDTH), f32)
        keep, send = call(
            functools.partial(project_body, tile, len(weights)),
            [half, half],
            (tokens, *near, *weights),
            [VMEM] * (4 + len(weights)),
            [pltpu.VMEM((SIDE * BLOCK, depth), bf16)],
            flops=2 * SIDE * BLOCK * depth * columns,
            moved=2 * depth * columns,
        )
        got = lax.ppermute(send, "gy", [(p, p ^ 1) for p in range(SIDE)])
        summed = keep[1] + got[1]
        sums += [keep, got, lax.ppermute(summed, "gy", [(p, p ^ 2) for p in range(SIDE)])]
    depth, out_width = w_output.shape
    part = out_width // 2
    stored_keys, stored_values, w_first, ready = fetch(
        [(stored_keys,), (stored_values,), (w_output, 0, part)], summed
    )
    piece = jax.ShapeDtypeStruct((ROWS * wide, HEAD_WIDTH), bf16)
    mine = call(
        functools.partial(spread_body, groups),
        [piece] * SIDE,
        (*sums, ready),
        [VMEM] * 7,
        [pltpu.VMEM((wide * BLOCK, HEAD_WIDTH), f32)],
    )
    others = partners(lambda k: mine[k], "gx")
    context = call(
        functools.partial(attend_body, groups),
        [piece] * SIDE,
        (lengths, mine[0], *others, cosine, sine, stored_keys, stored_values),
        [SMEM] + [VMEM] * 8,
        [pltpu.VMEM((SIDE, ROWS * wide, HEAD_WIDTH), bf16)],
    )
    others = partners(lambda k: context[k], "gy")
    rows = call(
        functools.partial(turn_body, groups),
        jax.ShapeDtypeStruct((BLOCK, groups * GROUP * HEAD_WIDTH), bf16),
        (context[0], *others),
        [VMEM] * 4,
        [pltpu.VMEM((SIDE * ROWS * wide, HEAD_WIDTH), f32)],
    )
    near = partners(lambda k: rows, "gx")
    w_second, _ = fetch([(w_output, part, part)], rows)
    half = jax.ShapeDtypeStruct((2 * BLOCK, out_width), f32)
    keep, send = call(
        functools.partial(output_body, tile),
        [half, half],
        (rows, *near, w_first, w_second),
        [VMEM] * 6,
        [pltpu.VMEM((SIDE * BLOCK, depth), bf16)] * 2,
        flops=2 * SIDE * BLOCK * depth * out_width,
        moved=2 * depth * out_width,
    )
    got = lax.ppermute(send, "gy", [(p, p ^ 1) for p in range(SIDE)])
    across = lax.ppermute(
        (keep[BLOCK:] + got[BLOCK:]).astype(bf16), "gy", [(p, p ^ 2) for p in range(SIDE)]
    )
    return ((keep[:BLOCK] + got[:BLOCK]) + across).astype(bf16)


def shards(*args):
    tokens, w_query, key_matrix, _, w_output, stored_keys, _, lengths, _ = args
    whole_heads = w_query.shape[1] % (GROUP * HEAD_WIDTH) == 0
    groups = key_matrix.shape[1] // HEAD_WIDTH
    square = (
        lax.axis_size("gx") == SIDE
        and lax.axis_size("gy") == SIDE
        and lengths.shape[0] == ROWS
        and tokens.shape[0] == BLOCK
        and whole_heads
        and groups * HEAD_WIDTH == key_matrix.shape[1]
        and groups * GROUP * HEAD_WIDTH == w_query.shape[1] == w_output.shape[0]
        and w_output.shape[1] % 1024 == 0
        and w_query.shape[1] % 1024 == 0
    )
    return square_shards(*args) if square else general_shards(*args)


def solution(mesh):
    in_specs = (
        P(("parts", "gx"), "gy"),
        P("gy", "gx"),
        P("gy", "gx"),
        P("gy", "gx"),
        P("gy", "gx"),
        P(("parts", "gy", "gx"), None, None),
        P(("parts", "gy", "gx"), None, None),
        P(("parts", "gy", "gx")),
        P(("parts", "gy", "gx")),
    )
    out_specs = P(("parts", "gy"), "gx")
    return jax.shard_map(shards, mesh=mesh, in_specs=in_specs, out_specs=out_specs, check_vma=False)
```

```python
import functools
import math

import jax
import jax.numpy as jnp
from jax import lax
from jax.experimental import pallas as pl
from jax.experimental.pallas import tpu as pltpu
from jax.sharding import PartitionSpec as P

QUERY_HEADS = 96
KEY_VALUE_HEADS = 8
HEAD_WIDTH = 128
CONTEXT_LENGTH = 128
GROUP = QUERY_HEADS // KEY_VALUE_HEADS


rope_theta = 1000000.0

VMEM = pl.BlockSpec(memory_space=pltpu.VMEM)
SMEM = pl.BlockSpec(memory_space=pltpu.SMEM)


def rotary_angles(positions):
    half_dim = HEAD_WIDTH // 2
    frequency = rope_theta ** (-(jnp.arange(half_dim, dtype=jnp.float32) * 2.0) / HEAD_WIDTH)
    return positions.astype(jnp.float32)[:, None] * frequency[None, :]


def rotary_table(values, positions, heads):
    number_rows = values.shape[0]
    head_size = values.shape[1] // heads
    half_dim = head_size // 2
    wide = values.astype(jnp.float32).reshape(number_rows, heads, head_size)
    angles = rotary_angles(positions)
    cosine = jnp.cos(angles)[:, None, :]
    sine = jnp.sin(angles)[:, None, :]
    lower_half = wide[..., :half_dim]
    upper_half = wide[..., half_dim:]
    turned = jnp.concatenate(
        [lower_half * cosine - upper_half * sine, upper_half * cosine + lower_half * sine], axis=-1
    )
    return turned.reshape(values.shape).astype(jnp.bfloat16)


def attend(rotated_query, rotated_key, fresh_value, device_keys, device_values, lengths):
    number_rows = rotated_query.shape[0]
    logit_scale = 1.0 / HEAD_WIDTH**0.5
    per_head_queries = rotated_query.reshape(number_rows, KEY_VALUE_HEADS, GROUP, HEAD_WIDTH)
    per_head_keys = device_keys.reshape(number_rows, CONTEXT_LENGTH, KEY_VALUE_HEADS, HEAD_WIDTH)
    scores = (
        jnp.einsum(
            "rgqd,rpgd->rgqp", per_head_queries, per_head_keys, preferred_element_type=jnp.float32
        )
        * logit_scale
    )
    live_mask = (jnp.arange(CONTEXT_LENGTH, dtype=jnp.int32)[None, :] < lengths[:, None])[
        :, None, None, :
    ]
    scores = jnp.where(live_mask, scores, -jnp.inf)
    self_score = (
        jnp.einsum(
            "uojn,uon->uoj",
            per_head_queries,
            rotated_key.reshape(number_rows, KEY_VALUE_HEADS, HEAD_WIDTH),
            preferred_element_type=jnp.float32,
        )
        * logit_scale
    )
    row_max = jnp.maximum(jnp.max(scores, axis=-1), self_score)
    cached_exp = jnp.exp(scores - row_max[..., None])
    own_exp = jnp.exp(self_score - row_max)
    totals = jnp.sum(cached_exp, axis=-1) + own_exp
    weights = (cached_exp / totals[..., None]).astype(jnp.bfloat16)
    self_weight = (own_exp / totals).astype(jnp.bfloat16)
    per_head_values = device_values.reshape(
        number_rows, CONTEXT_LENGTH, KEY_VALUE_HEADS, HEAD_WIDTH
    )
    context_window = jnp.einsum(
        "rgqp,rpgd->rgqd", weights, per_head_values, preferred_element_type=jnp.float32
    )
    context_window = context_window + self_weight.astype(jnp.float32)[
        ..., None
    ] * fresh_value.astype(jnp.float32).reshape(number_rows, KEY_VALUE_HEADS, 1, HEAD_WIDTH)
    return context_window.reshape(number_rows, QUERY_HEADS * HEAD_WIDTH).astype(jnp.bfloat16)


def general_shards(
    tokens,
    w_query,
    key_matrix,
    value_matrix,
    w_output,
    stored_keys,
    stored_values,
    lengths,
    positions,
):
    q_width = w_query.shape[1]
    kv_width = key_matrix.shape[1]
    piece = lax.all_gather(tokens, "gx", axis=0, tiled=True)
    partials = jnp.concatenate(
        [
            jnp.dot(piece, w_query, preferred_element_type=jnp.float32),
            jnp.dot(piece, key_matrix, preferred_element_type=jnp.float32),
            jnp.dot(piece, value_matrix, preferred_element_type=jnp.float32),
        ],
        axis=1,
    )
    summed = lax.psum_scatter(partials, "gy", scatter_dimension=0, tiled=True)
    query = summed[:, :q_width].astype(jnp.bfloat16)
    fresh_key = summed[:, q_width : q_width + kv_width].astype(jnp.bfloat16)
    fresh_value = summed[:, q_width + kv_width :].astype(jnp.bfloat16)
    query_rows, key_row_matrix, value_rows = (
        lax.all_to_all(query, "gx", split_axis=0, concat_axis=1, tiled=True),
        lax.all_to_all(fresh_key, "gx", split_axis=0, concat_axis=1, tiled=True),
        lax.all_to_all(fresh_value, "gx", split_axis=0, concat_axis=1, tiled=True),
    )
    rotated_query = rotary_table(query_rows, positions, QUERY_HEADS)
    rotated_key = rotary_table(key_row_matrix, positions, KEY_VALUE_HEADS)
    context_window = attend(
        rotated_query, rotated_key, value_rows, stored_keys, stored_values, lengths
    )
    out_width = w_output.shape[1]
    block_list = lax.all_to_all(context_window[None], "gy", split_axis=2, concat_axis=0, tiled=True)
    products = jnp.einsum(
        "jrd,de->jre",
        lax.all_gather(block_list, "gx", axis=1, tiled=True),
        w_output,
        preferred_element_type=jnp.float32,
    )
    products = products.reshape(-1, out_width)
    result = lax.psum_scatter(products, "gy", scatter_dimension=0, tiled=True)
    return result.astype(jnp.bfloat16)


SIDE = 4
ROWS = 4
BLOCK = SIDE * ROWS
SLOTS = 16
FROM = (0, 3, 1, 2)
HEADS_FROM = (0, 2, 3, 1)
CONTEXT_FROM = (0, 2, 3, 1)


def call(body, outs, args, specs, scratch=(), limit=8, flops=0, moved=0):
    return pl.pallas_call(
        body,
        out_shape=outs,
        in_specs=specs,
        out_specs=jax.tree.map(lambda _: VMEM, outs),
        scratch_shapes=list(scratch),
        compiler_params=pltpu.CompilerParams(vmem_limit_bytes=limit << 20),
        cost_estimate=pl.CostEstimate(flops=flops, bytes_accessed=moved, transcendentals=0),
    )(*args)


def fetch_body(parts, *refs):
    sems, done = refs[-1], refs[-2]
    targets = refs[-2 - len(parts) : -2]
    copies = []
    for n, (source, index, pieces) in enumerate(parts):
        size = refs[source].shape[0] // pieces
        for k in range(pieces):
            at = pl.ds(k * size, size)
            copies.append(
                pltpu.make_async_copy(
                    refs[source].at[(at, *index)], targets[n].at[at], sems.at[len(copies)]
                )
            )
    for copy in copies:
        copy.start()
    done[...] = jnp.zeros_like(done)
    for copy in copies:
        copy.wait()


def fetch(parts, *after):
    sources, plan, outs = [], [], []
    for array, *columns in parts:
        if not any(array is s for s in sources):
            sources.append(array)
        at = next(n for n, s in enumerate(sources) if s is array)
        index = (slice(None), pl.ds(*columns)) if columns else ()
        shape = (array.shape[0], columns[1]) if columns else array.shape
        plan.append((at, index[1:], 4))
        outs.append(pltpu.VMEM(shape, array.dtype))
    moved = 2 * sum(math.prod(out.shape) for out in outs)
    done = jax.ShapeDtypeStruct((8, HEAD_WIDTH), jnp.float32)
    return pl.pallas_call(
        functools.partial(fetch_body, plan),
        out_shape=[*outs, done],
        in_specs=[pl.BlockSpec(memory_space=pltpu.HBM)] * len(sources) + [VMEM] * len(after),
        out_specs=[VMEM] * (len(outs) + 1),
        scratch_shapes=[pltpu.SemaphoreType.DMA((4 * len(outs),))],
        compiler_params=pltpu.CompilerParams(vmem_limit_bytes=36 << 20),
        cost_estimate=pl.CostEstimate(flops=0, bytes_accessed=moved, transcendentals=0),
    )(*sources, *after)


def partners(block, axis, order):
    return [lax.ppermute(block(k), axis, [(p, p ^ k) for p in range(SIDE)]) for k in order[1:]]


def project_body(tile, count, x0, x1, x2, x3, *refs):
    weights = refs[:count]
    keep, send, rows = refs[count:]
    m = lax.axis_index("gx") ^ lax.axis_index("gy")
    for s, x in zip(FROM, (x0, x1, x2, x3)):
        d = s ^ m
        place = ((d & 1) << 1) | (d >> 1)
        rows[pl.ds(pl.multiple_of(place * BLOCK, BLOCK), BLOCK), :] = x[...]

    def put(w, c, width, head):
        acc = jnp.dot(rows[...], w[:, pl.ds(c, width)], preferred_element_type=jnp.float32)
        for k in range(width // HEAD_WIDTH):
            at = pl.ds(pl.multiple_of((head + k) * BLOCK, BLOCK), BLOCK)
            part = acc[:, k * HEAD_WIDTH : (k + 1) * HEAD_WIDTH]
            for b in range(2):
                keep[b, at, :] = part[b * BLOCK : (b + 1) * BLOCK]
                send[b, at, :] = part[(2 + b) * BLOCK : (3 + b) * BLOCK]

    head = 0
    for w in weights:
        width = min(tile, w.shape[1])
        per = width // HEAD_WIDTH

        def step(n, _):
            put(w, pl.multiple_of(n * width, width), width, head + n * per)
            return 0

        lax.fori_loop(0, w.shape[1] // width, step, 0)
        head += w.shape[1] // HEAD_WIDTH


def spread_body(groups, keep0, got0, across0, keep1, got1, across1, ready, *refs):
    outs, slots = refs[:-1], refs[-1]
    j = lax.axis_index("gx")
    first = keep0.shape[1] // BLOCK
    qh = groups * GROUP
    for g in range(groups):
        for u in range(SLOTS):
            if u < GROUP:
                h = g * GROUP + u
            elif u == GROUP:
                h = qh + g
            elif u == GROUP + 1:
                h = qh + groups + g
            else:
                h = None
            at = (g * SLOTS + u) * BLOCK
            if h is None:
                slots[at : at + BLOCK, :] = jnp.zeros((BLOCK, HEAD_WIDTH), jnp.float32)
                continue
            keep, got, across = (keep0, got0, across0) if h < first else (keep1, got1, across1)
            h = h if h < first else h - first
            src = slice(h * BLOCK, (h + 1) * BLOCK)
            total = (keep[0, src, :] + got[0, src, :]) + across[src, :]
            slots[at : at + BLOCK, :] = total.astype(jnp.bfloat16).astype(jnp.float32)
    wide = groups * SLOTS
    for e, out in enumerate(outs):
        for t in range(ROWS):
            row = (j ^ e) * ROWS + t
            out[t * wide : (t + 1) * wide, :] = slots[pl.ds(row, wide, stride=BLOCK), :].astype(
                jnp.bfloat16
            )


def attend_body(
    groups, lengths, a0, a1, a2, a3, cosine, sine, keys, values, c0, c1, c2, c3, held
):
    j = lax.axis_index("gx")
    m = j ^ lax.axis_index("gy")
    scale = 1.0 / HEAD_WIDTH**0.5
    wide = groups * SLOTS
    span = groups * HEAD_WIDTH
    slot = lax.broadcasted_iota(jnp.int32, (wide, HEAD_WIDTH), 0)
    is_value = slot % SLOTS == GROUP + 1
    of_group = [slot // SLOTS == g for g in range(groups)]
    spot = lax.broadcasted_iota(jnp.int32, (wide, CONTEXT_LENGTH), 1)
    pieces = [(e, t) for e in range(SIDE) for t in range(ROWS)]
    heads = dict(zip(HEADS_FROM, (a0, a1, a2, a3)))

    def lanes(e):
        return pl.ds(pl.multiple_of((j ^ e) * span, span), span)

    def each_group(block, row):
        out = block[row : row + 1]
        for g in range(1, groups):
            at = g * SLOTS + row
            out = jnp.where(of_group[g], block[at : at + 1], out)
        return out

    scores, owns, fresh = [], [], []
    for e, t in pieces:
        raw = heads[e][t * wide : (t + 1) * wide, :].astype(jnp.float32)
        turned = (
            raw * cosine[t : t + 1, :] + pltpu.roll(raw, HEAD_WIDTH // 2, 1) * sine[t : t + 1, :]
        )
        q = jnp.where(is_value, raw, turned).astype(jnp.bfloat16)
        wide_q = q.astype(jnp.float32)
        spread = jnp.concatenate(
            [jnp.where(of_group[g], wide_q, 0.0) for g in range(groups)], axis=1
        ).astype(jnp.bfloat16)
        found = lax.dot_general(
            spread,
            keys[t, :, lanes(e)],
            (((1,), (1,)), ((), ())),
            preferred_element_type=jnp.float32,
        )
        scores.append(jnp.where(spot < lengths[t], found * scale, -jnp.inf))
        owns.append(
            jnp.sum(wide_q * each_group(wide_q, GROUP), axis=1, keepdims=True) * scale
        )
        fresh.append(each_group(wide_q, GROUP + 1))
    tops = [
        jnp.maximum(jnp.max(s, axis=1, keepdims=True), own) for s, own in zip(scores, owns)
    ]
    cached = [jnp.exp(s - top) for s, top in zip(scores, tops)]
    owns = [jnp.exp(own - top) for own, top in zip(owns, tops)]
    totals = [jnp.sum(w, axis=1, keepdims=True) + own for w, own in zip(cached, owns)]
    weights = [(w / total).astype(jnp.bfloat16) for w, total in zip(cached, totals)]
    owns = [
        (own / total).astype(jnp.bfloat16).astype(jnp.float32) for own, total in zip(owns, totals)
    ]
    for n, (e, t) in enumerate(pieces):
        found = jnp.dot(weights[n], values[t, :, lanes(e)], preferred_element_type=jnp.float32)
        context = found[:, :HEAD_WIDTH]
        for g in range(1, groups):
            context = jnp.where(
                of_group[g], found[:, g * HEAD_WIDTH : (g + 1) * HEAD_WIDTH], context
            )
        context = context + owns[n] * fresh[n]
        held[e ^ m, t * wide : (t + 1) * wide, :] = context.astype(jnp.bfloat16)
    for f, c in enumerate((c0, c1, c2, c3)):
        c[...] = held[f]


def turn_body(groups, c0, c1, c2, c3, out, slots):
    i = lax.axis_index("gy")
    wide = groups * SLOTS
    size = ROWS * wide
    for f, c in zip(CONTEXT_FROM, (c0, c1, c2, c3)):
        slots[pl.ds(pl.multiple_of((i ^ f) * size, size), size), :] = c[...].astype(jnp.float32)
    for g in range(groups):
        for u in range(GROUP):
            h = g * GROUP + u
            out[:, h * HEAD_WIDTH : (h + 1) * HEAD_WIDTH] = slots[
                pl.ds(g * SLOTS + u, BLOCK, stride=wide), :
            ].astype(jnp.bfloat16)


def order_rows(blocks, rows, ordered):
    i, j = lax.axis_index("gy"), lax.axis_index("gx")
    for s, x in zip(FROM, blocks):
        rows[pl.ds(pl.multiple_of((j ^ s) * BLOCK, BLOCK), BLOCK), :] = x[...]
    count = SIDE * BLOCK
    r = lax.broadcasted_iota(jnp.int32, (count, count), 0)
    c = lax.broadcasted_iota(jnp.int32, (count, count), 1)
    place = r >> 4
    owner = i ^ (((place & 1) << 1) | (place >> 1))
    wanted = ((r & 12) << 2) | (owner << 2) | (r & 3)
    swap = jnp.where(c == wanted, 1.0, 0.0).astype(jnp.bfloat16)
    ordered[...] = jnp.dot(swap, rows[...], preferred_element_type=jnp.float32).astype(
        jnp.bfloat16
    )


def multiply(tile, ordered, w, keep, send):
    def step(n, _):
        at = pl.ds(pl.multiple_of(n * tile, tile), tile)
        acc = jnp.dot(ordered[...], w[:, at], preferred_element_type=jnp.float32)
        keep[:, at] = acc[: 2 * BLOCK]
        send[:, at] = acc[2 * BLOCK :]
        return 0

    lax.fori_loop(0, w.shape[1] // tile, step, 0)


def first_output_body(tile, x0, x1, x2, x3, w, ready, keep, send, ordered, rows):
    order_rows((x0, x1, x2, x3), rows, ordered)
    multiply(tile, ordered, w, keep, send)


def finish_body(keep0, got0, across0, keep1, got1, across1, out):
    first = keep0.shape[1]
    for keep, got, across, at in (
        (keep0, got0, across0, slice(0, first)),
        (keep1, got1, across1, slice(first, None)),
    ):
        total = (keep[:BLOCK, :] + got[:BLOCK, :]) + across[...].astype(jnp.float32)
        out[:, at] = total.astype(jnp.bfloat16)


def square_shards(
    tokens,
    w_query,
    key_matrix,
    value_matrix,
    w_output,
    stored_keys,
    stored_values,
    lengths,
    positions,
):
    f32, bf16 = jnp.float32, jnp.bfloat16
    depth, q_width = w_query.shape
    kv_width = key_matrix.shape[1]
    groups = kv_width // HEAD_WIDTH
    wide = groups * SLOTS

    angles = rotary_angles(positions)
    cosine, sine = jnp.cos(angles), jnp.sin(angles)
    cosine = jnp.concatenate([cosine, cosine], axis=1)
    sine = jnp.concatenate([-sine, sine], axis=1)

    near = partners(lambda k: tokens, "gx", FROM)
    tile = 512
    part = q_width // 2
    w_first, w_second, key_matrix, value_matrix, _ = fetch(
        [(w_query, 0, part), (w_query, part, part), (key_matrix,), (value_matrix,)]
    )
    sums = []
    for weights in ((w_first,), (w_second, key_matrix, value_matrix)):
        columns = sum(w.shape[1] for w in weights)
        half = jax.ShapeDtypeStruct((2, columns // HEAD_WIDTH * BLOCK, HEAD_WIDTH), f32)
        keep, send = call(
            functools.partial(project_body, tile, len(weights)),
            [half, half],
            (tokens, *near, *weights),
            [VMEM] * (4 + len(weights)),
            [pltpu.VMEM((SIDE * BLOCK, depth), bf16)],
            flops=2 * SIDE * BLOCK * depth * columns,
            moved=2 * depth * columns,
        )
        got = lax.ppermute(send, "gy", [(p, p ^ 1) for p in range(SIDE)])
        summed = keep[1] + got[1]
        sums += [keep, got, lax.ppermute(summed, "gy", [(p, p ^ 2) for p in range(SIDE)])]
    depth, out_width = w_output.shape
    part = out_width // 2
    stored_keys, stored_values, w_first, ready = fetch(
        [(stored_keys,), (stored_values,), (w_output, 0, part)], summed
    )
    piece = jax.ShapeDtypeStruct((ROWS * wide, HEAD_WIDTH), bf16)
    mine = call(
        functools.partial(spread_body, groups),
        [piece] * SIDE,
        (*sums, ready),
        [VMEM] * 7,
        [pltpu.VMEM((wide * BLOCK, HEAD_WIDTH), f32)],
    )
    others = partners(lambda k: mine[k], "gx", HEADS_FROM)
    context = call(
        functools.partial(attend_body, groups),
        [piece] * SIDE,
        (lengths, mine[0], *others, cosine, sine, stored_keys, stored_values),
        [SMEM] + [VMEM] * 8,
        [pltpu.VMEM((SIDE, ROWS * wide, HEAD_WIDTH), bf16)],
    )
    others = partners(lambda k: context[k], "gy", CONTEXT_FROM)
    rows = call(
        functools.partial(turn_body, groups),
        jax.ShapeDtypeStruct((BLOCK, groups * GROUP * HEAD_WIDTH), bf16),
        (context[0], *others),
        [VMEM] * 4,
        [pltpu.VMEM((SIDE * ROWS * wide, HEAD_WIDTH), f32)],
    )
    near = partners(lambda k: rows, "gx", FROM)
    w_second, ready = fetch([(w_output, part, part)], rows)
    sums = []
    for w in (w_first, w_second):
        columns = w.shape[1]
        half = jax.ShapeDtypeStruct((2 * BLOCK, columns), f32)
        flops, moved = 2 * SIDE * BLOCK * depth * columns, 2 * depth * columns
        if not sums:
            keep, send, ordered = call(
                functools.partial(first_output_body, tile),
                [half, half, jax.ShapeDtypeStruct((SIDE * BLOCK, depth), bf16)],
                (rows, *near, w, ready),
                [VMEM] * 6,
                [pltpu.VMEM((SIDE * BLOCK, depth), bf16)],
                flops=flops,
                moved=moved,
            )
        else:
            keep, send = call(
                functools.partial(multiply, tile),
                [half, half],
                (ordered, w),
                [VMEM] * 2,
                flops=flops,
                moved=moved,
            )
        got = lax.ppermute(send, "gy", [(p, p ^ 1) for p in range(SIDE)])
        summed = (keep[BLOCK:] + got[BLOCK:]).astype(bf16)
        sums += [keep, got, lax.ppermute(summed, "gy", [(p, p ^ 2) for p in range(SIDE)])]
    return call(
        finish_body, jax.ShapeDtypeStruct((BLOCK, out_width), bf16), sums, [VMEM] * 6
    )


def shards(*args):
    tokens, w_query, key_matrix, _, w_output, stored_keys, _, lengths, _ = args
    whole_heads = w_query.shape[1] % (GROUP * HEAD_WIDTH) == 0
    groups = key_matrix.shape[1] // HEAD_WIDTH
    square = (
        lax.axis_size("gx") == SIDE
        and lax.axis_size("gy") == SIDE
        and lengths.shape[0] == ROWS
        and tokens.shape[0] == BLOCK
        and whole_heads
        and groups * HEAD_WIDTH == key_matrix.shape[1]
        and groups * GROUP * HEAD_WIDTH == w_query.shape[1] == w_output.shape[0]
        and w_output.shape[1] % 1024 == 0
        and w_query.shape[1] % 1024 == 0
    )
    return square_shards(*args) if square else general_shards(*args)


def solution(mesh):
    in_specs = (
        P(("parts", "gx"), "gy"),
        P("gy", "gx"),
        P("gy", "gx"),
        P("gy", "gx"),
        P("gy", "gx"),
        P(("parts", "gy", "gx"), None, None),
        P(("parts", "gy", "gx"), None, None),
        P(("parts", "gy", "gx")),
        P(("parts", "gy", "gx")),
    )
    out_specs = P(("parts", "gy"), "gx")
    return jax.shard_map(shards, mesh=mesh, in_specs=in_specs, out_specs=out_specs, check_vma=False)
```

```python
import functools
import math

import jax
import jax.numpy as jnp
from jax import lax
from jax.experimental import pallas as pl
from jax.experimental.pallas import tpu as pltpu
from jax.sharding import PartitionSpec as P

QUERY_HEADS = 96
KEY_VALUE_HEADS = 8
HEAD_WIDTH = 128
CONTEXT_LENGTH = 128
GROUP = QUERY_HEADS // KEY_VALUE_HEADS


rope_theta = 1000000.0

VMEM = pl.BlockSpec(memory_space=pltpu.VMEM)
SMEM = pl.BlockSpec(memory_space=pltpu.SMEM)


def rotary_angles(positions):
    half_dim = HEAD_WIDTH // 2
    frequency = rope_theta ** (-(jnp.arange(half_dim, dtype=jnp.float32) * 2.0) / HEAD_WIDTH)
    return positions.astype(jnp.float32)[:, None] * frequency[None, :]


def rotary_table(values, positions, heads):
    number_rows = values.shape[0]
    head_size = values.shape[1] // heads
    half_dim = head_size // 2
    wide = values.astype(jnp.float32).reshape(number_rows, heads, head_size)
    angles = rotary_angles(positions)
    cosine = jnp.cos(angles)[:, None, :]
    sine = jnp.sin(angles)[:, None, :]
    lower_half = wide[..., :half_dim]
    upper_half = wide[..., half_dim:]
    turned = jnp.concatenate(
        [lower_half * cosine - upper_half * sine, upper_half * cosine + lower_half * sine], axis=-1
    )
    return turned.reshape(values.shape).astype(jnp.bfloat16)


def attend(rotated_query, rotated_key, fresh_value, device_keys, device_values, lengths):
    number_rows = rotated_query.shape[0]
    logit_scale = 1.0 / HEAD_WIDTH**0.5
    per_head_queries = rotated_query.reshape(number_rows, KEY_VALUE_HEADS, GROUP, HEAD_WIDTH)
    per_head_keys = device_keys.reshape(number_rows, CONTEXT_LENGTH, KEY_VALUE_HEADS, HEAD_WIDTH)
    scores = (
        jnp.einsum(
            "rgqd,rpgd->rgqp", per_head_queries, per_head_keys, preferred_element_type=jnp.float32
        )
        * logit_scale
    )
    live_mask = (jnp.arange(CONTEXT_LENGTH, dtype=jnp.int32)[None, :] < lengths[:, None])[
        :, None, None, :
    ]
    scores = jnp.where(live_mask, scores, -jnp.inf)
    self_score = (
        jnp.einsum(
            "uojn,uon->uoj",
            per_head_queries,
            rotated_key.reshape(number_rows, KEY_VALUE_HEADS, HEAD_WIDTH),
            preferred_element_type=jnp.float32,
        )
        * logit_scale
    )
    row_max = jnp.maximum(jnp.max(scores, axis=-1), self_score)
    cached_exp = jnp.exp(scores - row_max[..., None])
    own_exp = jnp.exp(self_score - row_max)
    totals = jnp.sum(cached_exp, axis=-1) + own_exp
    weights = (cached_exp / totals[..., None]).astype(jnp.bfloat16)
    self_weight = (own_exp / totals).astype(jnp.bfloat16)
    per_head_values = device_values.reshape(
        number_rows, CONTEXT_LENGTH, KEY_VALUE_HEADS, HEAD_WIDTH
    )
    context_window = jnp.einsum(
        "rgqp,rpgd->rgqd", weights, per_head_values, preferred_element_type=jnp.float32
    )
    context_window = context_window + self_weight.astype(jnp.float32)[
        ..., None
    ] * fresh_value.astype(jnp.float32).reshape(number_rows, KEY_VALUE_HEADS, 1, HEAD_WIDTH)
    return context_window.reshape(number_rows, QUERY_HEADS * HEAD_WIDTH).astype(jnp.bfloat16)


def general_shards(
    tokens,
    w_query,
    key_matrix,
    value_matrix,
    w_output,
    stored_keys,
    stored_values,
    lengths,
    positions,
):
    q_width = w_query.shape[1]
    kv_width = key_matrix.shape[1]
    piece = lax.all_gather(tokens, "gx", axis=0, tiled=True)
    partials = jnp.concatenate(
        [
            jnp.dot(piece, w_query, preferred_element_type=jnp.float32),
            jnp.dot(piece, key_matrix, preferred_element_type=jnp.float32),
            jnp.dot(piece, value_matrix, preferred_element_type=jnp.float32),
        ],
        axis=1,
    )
    summed = lax.psum_scatter(partials, "gy", scatter_dimension=0, tiled=True)
    query = summed[:, :q_width].astype(jnp.bfloat16)
    fresh_key = summed[:, q_width : q_width + kv_width].astype(jnp.bfloat16)
    fresh_value = summed[:, q_width + kv_width :].astype(jnp.bfloat16)
    query_rows, key_row_matrix, value_rows = (
        lax.all_to_all(query, "gx", split_axis=0, concat_axis=1, tiled=True),
        lax.all_to_all(fresh_key, "gx", split_axis=0, concat_axis=1, tiled=True),
        lax.all_to_all(fresh_value, "gx", split_axis=0, concat_axis=1, tiled=True),
    )
    rotated_query = rotary_table(query_rows, positions, QUERY_HEADS)
    rotated_key = rotary_table(key_row_matrix, positions, KEY_VALUE_HEADS)
    context_window = attend(
        rotated_query, rotated_key, value_rows, stored_keys, stored_values, lengths
    )
    out_width = w_output.shape[1]
    block_list = lax.all_to_all(context_window[None], "gy", split_axis=2, concat_axis=0, tiled=True)
    products = jnp.einsum(
        "jrd,de->jre",
        lax.all_gather(block_list, "gx", axis=1, tiled=True),
        w_output,
        preferred_element_type=jnp.float32,
    )
    products = products.reshape(-1, out_width)
    result = lax.psum_scatter(products, "gy", scatter_dimension=0, tiled=True)
    return result.astype(jnp.bfloat16)


SIDE = 4
ROWS = 4
BLOCK = SIDE * ROWS
SLOTS = 16
TOKENS_FROM = (0, 1, 2, 3)
FROM = (0, 3, 1, 2)
HEADS_FROM = (0, 2, 3, 1)
CONTEXT_FROM = (0, 2, 3, 1)


def call(body, outs, args, specs, scratch=(), limit=8, flops=0, moved=0):
    return pl.pallas_call(
        body,
        out_shape=outs,
        in_specs=specs,
        out_specs=jax.tree.map(lambda _: VMEM, outs),
        scratch_shapes=list(scratch),
        compiler_params=pltpu.CompilerParams(vmem_limit_bytes=limit << 20),
        cost_estimate=pl.CostEstimate(flops=flops, bytes_accessed=moved, transcendentals=0),
    )(*args)


def fetch_body(parts, *refs):
    sems, done = refs[-1], refs[-2]
    targets = refs[-2 - len(parts) : -2]
    copies = []
    for n, (source, index, pieces) in enumerate(parts):
        size = refs[source].shape[0] // pieces
        for k in range(pieces):
            at = pl.ds(k * size, size)
            copies.append(
                pltpu.make_async_copy(
                    refs[source].at[(at, *index)], targets[n].at[at], sems.at[len(copies)]
                )
            )
    for copy in copies:
        copy.start()
    done[...] = jnp.zeros_like(done)
    for copy in copies:
        copy.wait()


def fetch(parts, *after):
    sources, plan, outs = [], [], []
    for array, *columns in parts:
        if not any(array is s for s in sources):
            sources.append(array)
        at = next(n for n, s in enumerate(sources) if s is array)
        index = (slice(None), pl.ds(*columns)) if columns else ()
        shape = (array.shape[0], columns[1]) if columns else array.shape
        plan.append((at, index[1:], 4))
        outs.append(pltpu.VMEM(shape, array.dtype))
    moved = 2 * sum(math.prod(out.shape) for out in outs)
    done = jax.ShapeDtypeStruct((8, HEAD_WIDTH), jnp.float32)
    return pl.pallas_call(
        functools.partial(fetch_body, plan),
        out_shape=[*outs, done],
        in_specs=[pl.BlockSpec(memory_space=pltpu.HBM)] * len(sources) + [VMEM] * len(after),
        out_specs=[VMEM] * (len(outs) + 1),
        scratch_shapes=[pltpu.SemaphoreType.DMA((4 * len(outs),))],
        compiler_params=pltpu.CompilerParams(vmem_limit_bytes=36 << 20),
        cost_estimate=pl.CostEstimate(flops=0, bytes_accessed=moved, transcendentals=0),
    )(*sources, *after)


def partners(block, axis, order):
    return [lax.ppermute(block(k), axis, [(p, p ^ k) for p in range(SIDE)]) for k in order[1:]]


def project_body(tile, count, x0, x1, x2, x3, *refs):
    weights = refs[:count]
    keep, send, rows = refs[count:]
    m = lax.axis_index("gx") ^ lax.axis_index("gy")
    for s, x in zip(TOKENS_FROM, (x0, x1, x2, x3)):
        d = s ^ m
        place = ((d & 1) << 1) | (d >> 1)
        rows[pl.ds(pl.multiple_of(place * BLOCK, BLOCK), BLOCK), :] = x[...]

    def put(w, c, width, head):
        acc = jnp.dot(rows[...], w[:, pl.ds(c, width)], preferred_element_type=jnp.float32)
        for k in range(width // HEAD_WIDTH):
            at = pl.ds(pl.multiple_of((head + k) * BLOCK, BLOCK), BLOCK)
            part = acc[:, k * HEAD_WIDTH : (k + 1) * HEAD_WIDTH]
            for b in range(2):
                keep[b, at, :] = part[b * BLOCK : (b + 1) * BLOCK]
                send[b, at, :] = part[(2 + b) * BLOCK : (3 + b) * BLOCK]

    head = 0
    for w in weights:
        width = min(tile, w.shape[1])
        per = width // HEAD_WIDTH

        def step(n, _):
            put(w, pl.multiple_of(n * width, width), width, head + n * per)
            return 0

        lax.fori_loop(0, w.shape[1] // width, step, 0)
        head += w.shape[1] // HEAD_WIDTH


def spread_body(groups, keep0, got0, across0, keep1, got1, across1, ready, *refs):
    outs, slots = refs[:-1], refs[-1]
    j = lax.axis_index("gx")
    first = keep0.shape[1] // BLOCK
    qh = groups * GROUP
    for g in range(groups):
        for u in range(SLOTS):
            if u < GROUP:
                h = g * GROUP + u
            elif u == GROUP:
                h = qh + g
            elif u == GROUP + 1:
                h = qh + groups + g
            else:
                h = None
            at = (g * SLOTS + u) * BLOCK
            if h is None:
                slots[at : at + BLOCK, :] = jnp.zeros((BLOCK, HEAD_WIDTH), jnp.float32)
                continue
            keep, got, across = (keep0, got0, across0) if h < first else (keep1, got1, across1)
            h = h if h < first else h - first
            src = slice(h * BLOCK, (h + 1) * BLOCK)
            total = (keep[0, src, :] + got[0, src, :]) + across[src, :]
            slots[at : at + BLOCK, :] = total.astype(jnp.bfloat16).astype(jnp.float32)
    wide = groups * SLOTS
    for e, out in enumerate(outs):
        for t in range(ROWS):
            row = (j ^ e) * ROWS + t
            out[t * wide : (t + 1) * wide, :] = slots[pl.ds(row, wide, stride=BLOCK), :].astype(
                jnp.bfloat16
            )


def attend_body(
    groups, lengths, a0, a1, a2, a3, cosine, sine, keys, values, c0, c1, c2, c3, held
):
    j = lax.axis_index("gx")
    m = j ^ lax.axis_index("gy")
    scale = 1.0 / HEAD_WIDTH**0.5
    wide = groups * SLOTS
    span = groups * HEAD_WIDTH
    slot = lax.broadcasted_iota(jnp.int32, (wide, HEAD_WIDTH), 0)
    is_value = slot % SLOTS == GROUP + 1
    of_group = [slot // SLOTS == g for g in range(groups)]
    spot = lax.broadcasted_iota(jnp.int32, (wide, CONTEXT_LENGTH), 1)
    pieces = [(e, t) for e in range(SIDE) for t in range(ROWS)]
    heads = dict(zip(HEADS_FROM, (a0, a1, a2, a3)))

    def lanes(e):
        return pl.ds(pl.multiple_of((j ^ e) * span, span), span)

    def each_group(block, row):
        out = block[row : row + 1]
        for g in range(1, groups):
            at = g * SLOTS + row
            out = jnp.where(of_group[g], block[at : at + 1], out)
        return out

    scores, owns, fresh = [], [], []
    for e, t in pieces:
        raw = heads[e][t * wide : (t + 1) * wide, :].astype(jnp.float32)
        turned = (
            raw * cosine[t : t + 1, :] + pltpu.roll(raw, HEAD_WIDTH // 2, 1) * sine[t : t + 1, :]
        )
        q = jnp.where(is_value, raw, turned).astype(jnp.bfloat16)
        wide_q = q.astype(jnp.float32)
        spread = jnp.concatenate(
            [jnp.where(of_group[g], wide_q, 0.0) for g in range(groups)], axis=1
        ).astype(jnp.bfloat16)
        found = lax.dot_general(
            spread,
            keys[t, :, lanes(e)],
            (((1,), (1,)), ((), ())),
            preferred_element_type=jnp.float32,
        )
        scores.append(jnp.where(spot < lengths[t], found * scale, -jnp.inf))
        owns.append(
            jnp.sum(wide_q * each_group(wide_q, GROUP), axis=1, keepdims=True) * scale
        )
        fresh.append(each_group(wide_q, GROUP + 1))
    tops = [
        jnp.maximum(jnp.max(s, axis=1, keepdims=True), own) for s, own in zip(scores, owns)
    ]
    cached = [jnp.exp(s - top) for s, top in zip(scores, tops)]
    owns = [jnp.exp(own - top) for own, top in zip(owns, tops)]
    totals = [jnp.sum(w, axis=1, keepdims=True) + own for w, own in zip(cached, owns)]
    weights = [(w / total).astype(jnp.bfloat16) for w, total in zip(cached, totals)]
    owns = [
        (own / total).astype(jnp.bfloat16).astype(jnp.float32) for own, total in zip(owns, totals)
    ]
    for n, (e, t) in enumerate(pieces):
        found = jnp.dot(weights[n], values[t, :, lanes(e)], preferred_element_type=jnp.float32)
        context = found[:, :HEAD_WIDTH]
        for g in range(1, groups):
            context = jnp.where(
                of_group[g], found[:, g * HEAD_WIDTH : (g + 1) * HEAD_WIDTH], context
            )
        context = context + owns[n] * fresh[n]
        held[e ^ m, t * wide : (t + 1) * wide, :] = context.astype(jnp.bfloat16)
    for f, c in enumerate((c0, c1, c2, c3)):
        c[...] = held[f]


def turn_body(groups, c0, c1, c2, c3, out, slots):
    i = lax.axis_index("gy")
    wide = groups * SLOTS
    size = ROWS * wide
    for f, c in zip(CONTEXT_FROM, (c0, c1, c2, c3)):
        slots[pl.ds(pl.multiple_of((i ^ f) * size, size), size), :] = c[...].astype(jnp.float32)
    for g in range(groups):
        for u in range(GROUP):
            h = g * GROUP + u
            out[:, h * HEAD_WIDTH : (h + 1) * HEAD_WIDTH] = slots[
                pl.ds(g * SLOTS + u, BLOCK, stride=wide), :
            ].astype(jnp.bfloat16)


def order_rows(blocks, rows, ordered):
    i, j = lax.axis_index("gy"), lax.axis_index("gx")
    for s, x in zip(FROM, blocks):
        rows[pl.ds(pl.multiple_of((j ^ s) * BLOCK, BLOCK), BLOCK), :] = x[...]
    count = SIDE * BLOCK
    r = lax.broadcasted_iota(jnp.int32, (count, count), 0)
    c = lax.broadcasted_iota(jnp.int32, (count, count), 1)
    place = r >> 4
    owner = i ^ (((place & 1) << 1) | (place >> 1))
    wanted = ((r & 12) << 2) | (owner << 2) | (r & 3)
    swap = jnp.where(c == wanted, 1.0, 0.0).astype(jnp.bfloat16)
    ordered[...] = jnp.dot(swap, rows[...], preferred_element_type=jnp.float32).astype(
        jnp.bfloat16
    )


def multiply(tile, ordered, w, keep, send):
    def step(n, _):
        at = pl.ds(pl.multiple_of(n * tile, tile), tile)
        acc = jnp.dot(ordered[...], w[:, at], preferred_element_type=jnp.float32)
        keep[:, at] = acc[: 2 * BLOCK]
        send[:, at] = acc[2 * BLOCK :]
        return 0

    lax.fori_loop(0, w.shape[1] // tile, step, 0)


def first_output_body(tile, x0, x1, x2, x3, w, ready, keep, send, ordered, rows):
    order_rows((x0, x1, x2, x3), rows, ordered)
    multiply(tile, ordered, w, keep, send)


def finish_body(keep0, got0, across0, keep1, got1, across1, out):
    first = keep0.shape[1]
    for keep, got, across, at in (
        (keep0, got0, across0, slice(0, first)),
        (keep1, got1, across1, slice(first, None)),
    ):
        total = (keep[:BLOCK, :] + got[:BLOCK, :]) + across[...].astype(jnp.float32)
        out[:, at] = total.astype(jnp.bfloat16)


def square_shards(
    tokens,
    w_query,
    key_matrix,
    value_matrix,
    w_output,
    stored_keys,
    stored_values,
    lengths,
    positions,
):
    f32, bf16 = jnp.float32, jnp.bfloat16
    depth, q_width = w_query.shape
    kv_width = key_matrix.shape[1]
    groups = kv_width // HEAD_WIDTH
    wide = groups * SLOTS

    angles = rotary_angles(positions)
    cosine, sine = jnp.cos(angles), jnp.sin(angles)
    cosine = jnp.concatenate([cosine, cosine], axis=1)
    sine = jnp.concatenate([-sine, sine], axis=1)

    near = partners(lambda k: tokens, "gx", TOKENS_FROM)
    tile = 512
    part = q_width // 2
    w_first, w_second, _ = fetch([(w_query, 0, part), (w_query, part, part)])
    sums = []
    for weights in ((w_first,), (w_second, key_matrix, value_matrix)):
        columns = sum(w.shape[1] for w in weights)
        half = jax.ShapeDtypeStruct((2, columns // HEAD_WIDTH * BLOCK, HEAD_WIDTH), f32)
        keep, send = call(
            functools.partial(project_body, tile, len(weights)),
            [half, half],
            (tokens, *near, *weights),
            [VMEM] * (4 + len(weights)),
            [pltpu.VMEM((SIDE * BLOCK, depth), bf16)],
            flops=2 * SIDE * BLOCK * depth * columns,
            moved=2 * depth * columns,
        )
        got = lax.ppermute(send, "gy", [(p, p ^ 1) for p in range(SIDE)])
        summed = keep[1] + got[1]
        sums += [keep, got, lax.ppermute(summed, "gy", [(p, p ^ 2) for p in range(SIDE)])]
    depth, out_width = w_output.shape
    part = out_width // 2
    stored_keys, stored_values, w_first, ready = fetch(
        [(stored_keys,), (stored_values,), (w_output, 0, part)], summed
    )
    piece = jax.ShapeDtypeStruct((ROWS * wide, HEAD_WIDTH), bf16)
    mine = call(
        functools.partial(spread_body, groups),
        [piece] * SIDE,
        (*sums, ready),
        [VMEM] * 7,
        [pltpu.VMEM((wide * BLOCK, HEAD_WIDTH), f32)],
    )
    others = partners(lambda k: mine[k], "gx", HEADS_FROM)
    context = call(
        functools.partial(attend_body, groups),
        [piece] * SIDE,
        (lengths, mine[0], *others, cosine, sine, stored_keys, stored_values),
        [SMEM] + [VMEM] * 8,
        [pltpu.VMEM((SIDE, ROWS * wide, HEAD_WIDTH), bf16)],
    )
    others = partners(lambda k: context[k], "gy", CONTEXT_FROM)
    rows = call(
        functools.partial(turn_body, groups),
        jax.ShapeDtypeStruct((BLOCK, groups * GROUP * HEAD_WIDTH), bf16),
        (context[0], *others),
        [VMEM] * 4,
        [pltpu.VMEM((SIDE * ROWS * wide, HEAD_WIDTH), f32)],
    )
    near = partners(lambda k: rows, "gx", FROM)
    w_second, ready = fetch([(w_output, part, part)], rows)
    sums = []
    for w in (w_first, w_second):
        columns = w.shape[1]
        half = jax.ShapeDtypeStruct((2 * BLOCK, columns), f32)
        flops, moved = 2 * SIDE * BLOCK * depth * columns, 2 * depth * columns
        if not sums:
            keep, send, ordered = call(
                functools.partial(first_output_body, tile),
                [half, half, jax.ShapeDtypeStruct((SIDE * BLOCK, depth), bf16)],
                (rows, *near, w, ready),
                [VMEM] * 6,
                [pltpu.VMEM((SIDE * BLOCK, depth), bf16)],
                flops=flops,
                moved=moved,
            )
        else:
            keep, send = call(
                functools.partial(multiply, tile),
                [half, half],
                (ordered, w),
                [VMEM] * 2,
                flops=flops,
                moved=moved,
            )
        got = lax.ppermute(send, "gy", [(p, p ^ 1) for p in range(SIDE)])
        summed = (keep[BLOCK:] + got[BLOCK:]).astype(bf16)
        sums += [keep, got, lax.ppermute(summed, "gy", [(p, p ^ 2) for p in range(SIDE)])]
    return call(
        finish_body, jax.ShapeDtypeStruct((BLOCK, out_width), bf16), sums, [VMEM] * 6
    )


def shards(*args):
    tokens, w_query, key_matrix, _, w_output, stored_keys, _, lengths, _ = args
    whole_heads = w_query.shape[1] % (GROUP * HEAD_WIDTH) == 0
    groups = key_matrix.shape[1] // HEAD_WIDTH
    square = (
        lax.axis_size("gx") == SIDE
        and lax.axis_size("gy") == SIDE
        and lengths.shape[0] == ROWS
        and tokens.shape[0] == BLOCK
        and whole_heads
        and groups * HEAD_WIDTH == key_matrix.shape[1]
        and groups * GROUP * HEAD_WIDTH == w_query.shape[1] == w_output.shape[0]
        and w_output.shape[1] % 1024 == 0
        and w_query.shape[1] % 1024 == 0
    )
    return square_shards(*args) if square else general_shards(*args)


def solution(mesh):
    in_specs = (
        P(("parts", "gx"), "gy"),
        P("gy", "gx"),
        P("gy", "gx"),
        P("gy", "gx"),
        P("gy", "gx"),
        P(("parts", "gy", "gx"), None, None),
        P(("parts", "gy", "gx"), None, None),
        P(("parts", "gy", "gx")),
        P(("parts", "gy", "gx")),
    )
    out_specs = P(("parts", "gy"), "gx")
    return jax.shard_map(shards, mesh=mesh, in_specs=in_specs, out_specs=out_specs, check_vma=False)
```

```python
import functools
import math

import jax
import jax.numpy as jnp
from jax import lax
from jax.experimental import pallas as pl
from jax.experimental.pallas import tpu as pltpu
from jax.sharding import PartitionSpec as P

QUERY_HEADS = 96
KEY_VALUE_HEADS = 8
HEAD_WIDTH = 128
CONTEXT_LENGTH = 128
GROUP = QUERY_HEADS // KEY_VALUE_HEADS


rope_theta = 1000000.0

VMEM = pl.BlockSpec(memory_space=pltpu.VMEM)
SMEM = pl.BlockSpec(memory_space=pltpu.SMEM)


def rotary_angles(positions):
    half_dim = HEAD_WIDTH // 2
    frequency = rope_theta ** (-(jnp.arange(half_dim, dtype=jnp.float32) * 2.0) / HEAD_WIDTH)
    return positions.astype(jnp.float32)[:, None] * frequency[None, :]


def rotary_table(values, positions, heads):
    number_rows = values.shape[0]
    head_size = values.shape[1] // heads
    half_dim = head_size // 2
    wide = values.astype(jnp.float32).reshape(number_rows, heads, head_size)
    angles = rotary_angles(positions)
    cosine = jnp.cos(angles)[:, None, :]
    sine = jnp.sin(angles)[:, None, :]
    lower_half = wide[..., :half_dim]
    upper_half = wide[..., half_dim:]
    turned = jnp.concatenate(
        [lower_half * cosine - upper_half * sine, upper_half * cosine + lower_half * sine], axis=-1
    )
    return turned.reshape(values.shape).astype(jnp.bfloat16)


def attend(rotated_query, rotated_key, fresh_value, device_keys, device_values, lengths):
    number_rows = rotated_query.shape[0]
    logit_scale = 1.0 / HEAD_WIDTH**0.5
    per_head_queries = rotated_query.reshape(number_rows, KEY_VALUE_HEADS, GROUP, HEAD_WIDTH)
    per_head_keys = device_keys.reshape(number_rows, CONTEXT_LENGTH, KEY_VALUE_HEADS, HEAD_WIDTH)
    scores = (
        jnp.einsum(
            "rgqd,rpgd->rgqp", per_head_queries, per_head_keys, preferred_element_type=jnp.float32
        )
        * logit_scale
    )
    live_mask = (jnp.arange(CONTEXT_LENGTH, dtype=jnp.int32)[None, :] < lengths[:, None])[
        :, None, None, :
    ]
    scores = jnp.where(live_mask, scores, -jnp.inf)
    self_score = (
        jnp.einsum(
            "uojn,uon->uoj",
            per_head_queries,
            rotated_key.reshape(number_rows, KEY_VALUE_HEADS, HEAD_WIDTH),
            preferred_element_type=jnp.float32,
        )
        * logit_scale
    )
    row_max = jnp.maximum(jnp.max(scores, axis=-1), self_score)
    cached_exp = jnp.exp(scores - row_max[..., None])
    own_exp = jnp.exp(self_score - row_max)
    totals = jnp.sum(cached_exp, axis=-1) + own_exp
    weights = (cached_exp / totals[..., None]).astype(jnp.bfloat16)
    self_weight = (own_exp / totals).astype(jnp.bfloat16)
    per_head_values = device_values.reshape(
        number_rows, CONTEXT_LENGTH, KEY_VALUE_HEADS, HEAD_WIDTH
    )
    context_window = jnp.einsum(
        "rgqp,rpgd->rgqd", weights, per_head_values, preferred_element_type=jnp.float32
    )
    context_window = context_window + self_weight.astype(jnp.float32)[
        ..., None
    ] * fresh_value.astype(jnp.float32).reshape(number_rows, KEY_VALUE_HEADS, 1, HEAD_WIDTH)
    return context_window.reshape(number_rows, QUERY_HEADS * HEAD_WIDTH).astype(jnp.bfloat16)


def general_shards(
    tokens,
    w_query,
    key_matrix,
    value_matrix,
    w_output,
    stored_keys,
    stored_values,
    lengths,
    positions,
):
    q_width = w_query.shape[1]
    kv_width = key_matrix.shape[1]
    piece = lax.all_gather(tokens, "gx", axis=0, tiled=True)
    partials = jnp.concatenate(
        [
            jnp.dot(piece, w_query, preferred_element_type=jnp.float32),
            jnp.dot(piece, key_matrix, preferred_element_type=jnp.float32),
            jnp.dot(piece, value_matrix, preferred_element_type=jnp.float32),
        ],
        axis=1,
    )
    summed = lax.psum_scatter(partials, "gy", scatter_dimension=0, tiled=True)
    query = summed[:, :q_width].astype(jnp.bfloat16)
    fresh_key = summed[:, q_width : q_width + kv_width].astype(jnp.bfloat16)
    fresh_value = summed[:, q_width + kv_width :].astype(jnp.bfloat16)
    query_rows, key_row_matrix, value_rows = (
        lax.all_to_all(query, "gx", split_axis=0, concat_axis=1, tiled=True),
        lax.all_to_all(fresh_key, "gx", split_axis=0, concat_axis=1, tiled=True),
        lax.all_to_all(fresh_value, "gx", split_axis=0, concat_axis=1, tiled=True),
    )
    rotated_query = rotary_table(query_rows, positions, QUERY_HEADS)
    rotated_key = rotary_table(key_row_matrix, positions, KEY_VALUE_HEADS)
    context_window = attend(
        rotated_query, rotated_key, value_rows, stored_keys, stored_values, lengths
    )
    out_width = w_output.shape[1]
    block_list = lax.all_to_all(context_window[None], "gy", split_axis=2, concat_axis=0, tiled=True)
    products = jnp.einsum(
        "jrd,de->jre",
        lax.all_gather(block_list, "gx", axis=1, tiled=True),
        w_output,
        preferred_element_type=jnp.float32,
    )
    products = products.reshape(-1, out_width)
    result = lax.psum_scatter(products, "gy", scatter_dimension=0, tiled=True)
    return result.astype(jnp.bfloat16)


SIDE = 4
ROWS = 4
BLOCK = SIDE * ROWS
SLOTS = 16
TOKENS_FROM = (0, 1, 2, 3)
FROM = (0, 3, 1, 2)
HEADS_FROM = (0, 2, 3, 1)
CONTEXT_FROM = (0, 2, 3, 1)


def call(body, outs, args, specs, scratch=(), limit=8, flops=0, moved=0):
    return pl.pallas_call(
        body,
        out_shape=outs,
        in_specs=specs,
        out_specs=jax.tree.map(lambda _: VMEM, outs),
        scratch_shapes=list(scratch),
        compiler_params=pltpu.CompilerParams(vmem_limit_bytes=limit << 20),
        cost_estimate=pl.CostEstimate(flops=flops, bytes_accessed=moved, transcendentals=0),
    )(*args)


def fetch_body(parts, *refs):
    sems, done = refs[-1], refs[-2]
    targets = refs[-2 - len(parts) : -2]
    copies = []
    for n, (source, index, pieces) in enumerate(parts):
        size = refs[source].shape[0] // pieces
        for k in range(pieces):
            at = pl.ds(k * size, size)
            copies.append(
                pltpu.make_async_copy(
                    refs[source].at[(at, *index)], targets[n].at[at], sems.at[len(copies)]
                )
            )
    for copy in copies:
        copy.start()
    done[...] = jnp.zeros_like(done)
    for copy in copies:
        copy.wait()


def fetch(parts, *after):
    sources, plan, outs = [], [], []
    for array, *columns in parts:
        if not any(array is s for s in sources):
            sources.append(array)
        at = next(n for n, s in enumerate(sources) if s is array)
        index = (slice(None), pl.ds(*columns)) if columns else ()
        shape = (array.shape[0], columns[1]) if columns else array.shape
        plan.append((at, index[1:], 4))
        outs.append(pltpu.VMEM(shape, array.dtype))
    moved = 2 * sum(math.prod(out.shape) for out in outs)
    done = jax.ShapeDtypeStruct((8, HEAD_WIDTH), jnp.float32)
    return pl.pallas_call(
        functools.partial(fetch_body, plan),
        out_shape=[*outs, done],
        in_specs=[pl.BlockSpec(memory_space=pltpu.HBM)] * len(sources) + [VMEM] * len(after),
        out_specs=[VMEM] * (len(outs) + 1),
        scratch_shapes=[pltpu.SemaphoreType.DMA((4 * len(outs),))],
        compiler_params=pltpu.CompilerParams(vmem_limit_bytes=36 << 20),
        cost_estimate=pl.CostEstimate(flops=0, bytes_accessed=moved, transcendentals=0),
    )(*sources, *after)


def partners(block, axis, order):
    return [lax.ppermute(block(k), axis, [(p, p ^ k) for p in range(SIDE)]) for k in order[1:]]


def project_body(tile, count, x0, x1, x2, x3, *refs):
    weights = refs[:count]
    keep, send, rows = refs[count:]
    m = lax.axis_index("gx") ^ lax.axis_index("gy")
    for s, x in zip(TOKENS_FROM, (x0, x1, x2, x3)):
        d = s ^ m
        place = ((d & 1) << 1) | (d >> 1)
        rows[pl.ds(pl.multiple_of(place * BLOCK, BLOCK), BLOCK), :] = x[...]

    def put(w, c, width, head):
        acc = jnp.dot(rows[...], w[:, pl.ds(c, width)], preferred_element_type=jnp.float32)
        for k in range(width // HEAD_WIDTH):
            at = pl.ds(pl.multiple_of((head + k) * BLOCK, BLOCK), BLOCK)
            part = acc[:, k * HEAD_WIDTH : (k + 1) * HEAD_WIDTH]
            for b in range(2):
                keep[b, at, :] = part[b * BLOCK : (b + 1) * BLOCK]
                send[b, at, :] = part[(2 + b) * BLOCK : (3 + b) * BLOCK]

    head = 0
    for w in weights:
        width = min(tile, w.shape[1])
        per = width // HEAD_WIDTH

        def step(n, _):
            put(w, pl.multiple_of(n * width, width), width, head + n * per)
            return 0

        lax.fori_loop(0, w.shape[1] // width, step, 0)
        head += w.shape[1] // HEAD_WIDTH


def spread_body(groups, keep0, got0, across0, keep1, got1, across1, ready, *refs):
    outs, slots = refs[:-1], refs[-1]
    j = lax.axis_index("gx")
    first = keep0.shape[1] // BLOCK
    qh = groups * GROUP
    for g in range(groups):
        for u in range(SLOTS):
            if u < GROUP:
                h = g * GROUP + u
            elif u == GROUP:
                h = qh + g
            elif u == GROUP + 1:
                h = qh + groups + g
            else:
                h = None
            at = (g * SLOTS + u) * BLOCK
            if h is None:
                slots[at : at + BLOCK, :] = jnp.zeros((BLOCK, HEAD_WIDTH), jnp.float32)
                continue
            keep, got, across = (keep0, got0, across0) if h < first else (keep1, got1, across1)
            h = h if h < first else h - first
            src = slice(h * BLOCK, (h + 1) * BLOCK)
            total = (keep[0, src, :] + got[0, src, :]) + across[src, :]
            slots[at : at + BLOCK, :] = total.astype(jnp.bfloat16).astype(jnp.float32)
    wide = groups * SLOTS
    for e, out in enumerate(outs):
        for t in range(ROWS):
            row = (j ^ e) * ROWS + t
            out[t * wide : (t + 1) * wide, :] = slots[pl.ds(row, wide, stride=BLOCK), :].astype(
                jnp.bfloat16
            )


def attend_body(
    groups, lengths, a0, a1, a2, a3, cosine, sine, keys, values, c0, c1, c2, c3, held
):
    j = lax.axis_index("gx")
    m = j ^ lax.axis_index("gy")
    scale = 1.0 / HEAD_WIDTH**0.5
    wide = groups * SLOTS
    span = groups * HEAD_WIDTH
    slot = lax.broadcasted_iota(jnp.int32, (wide, HEAD_WIDTH), 0)
    is_value = slot % SLOTS == GROUP + 1
    of_group = [slot // SLOTS == g for g in range(groups)]
    spot = lax.broadcasted_iota(jnp.int32, (wide, CONTEXT_LENGTH), 1)
    pieces = [(e, t) for e in range(SIDE) for t in range(ROWS)]
    heads = dict(zip(HEADS_FROM, (a0, a1, a2, a3)))

    def lanes(e):
        return pl.ds(pl.multiple_of((j ^ e) * span, span), span)

    def each_group(block, row):
        out = block[row : row + 1]
        for g in range(1, groups):
            at = g * SLOTS + row
            out = jnp.where(of_group[g], block[at : at + 1], out)
        return out

    scores, owns, fresh = [], [], []
    for e, t in pieces:
        raw = heads[e][t * wide : (t + 1) * wide, :].astype(jnp.float32)
        turned = (
            raw * cosine[t : t + 1, :] + pltpu.roll(raw, HEAD_WIDTH // 2, 1) * sine[t : t + 1, :]
        )
        q = jnp.where(is_value, raw, turned).astype(jnp.bfloat16)
        wide_q = q.astype(jnp.float32)
        spread = jnp.concatenate(
            [jnp.where(of_group[g], wide_q, 0.0) for g in range(groups)], axis=1
        ).astype(jnp.bfloat16)
        found = lax.dot_general(
            spread,
            keys[t, :, lanes(e)],
            (((1,), (1,)), ((), ())),
            preferred_element_type=jnp.float32,
        )
        scores.append(jnp.where(spot < lengths[t], found * scale, -jnp.inf))
        owns.append(
            jnp.sum(wide_q * each_group(wide_q, GROUP), axis=1, keepdims=True) * scale
        )
        fresh.append(each_group(wide_q, GROUP + 1))
    tops = [
        jnp.maximum(jnp.max(s, axis=1, keepdims=True), own) for s, own in zip(scores, owns)
    ]
    cached = [jnp.exp(s - top) for s, top in zip(scores, tops)]
    owns = [jnp.exp(own - top) for own, top in zip(owns, tops)]
    totals = [jnp.sum(w, axis=1, keepdims=True) + own for w, own in zip(cached, owns)]
    weights = [(w / total).astype(jnp.bfloat16) for w, total in zip(cached, totals)]
    owns = [
        (own / total).astype(jnp.bfloat16).astype(jnp.float32) for own, total in zip(owns, totals)
    ]
    for n, (e, t) in enumerate(pieces):
        found = jnp.dot(weights[n], values[t, :, lanes(e)], preferred_element_type=jnp.float32)
        context = found[:, :HEAD_WIDTH]
        for g in range(1, groups):
            context = jnp.where(
                of_group[g], found[:, g * HEAD_WIDTH : (g + 1) * HEAD_WIDTH], context
            )
        context = context + owns[n] * fresh[n]
        held[e ^ m, t * wide : (t + 1) * wide, :] = context.astype(jnp.bfloat16)
    for f, c in enumerate((c0, c1, c2, c3)):
        c[...] = held[f]


def turn_body(groups, c0, c1, c2, c3, out, slots):
    i = lax.axis_index("gy")
    wide = groups * SLOTS
    size = ROWS * wide
    for f, c in zip(CONTEXT_FROM, (c0, c1, c2, c3)):
        slots[pl.ds(pl.multiple_of((i ^ f) * size, size), size), :] = c[...].astype(jnp.float32)
    for g in range(groups):
        for u in range(GROUP):
            h = g * GROUP + u
            out[:, h * HEAD_WIDTH : (h + 1) * HEAD_WIDTH] = slots[
                pl.ds(g * SLOTS + u, BLOCK, stride=wide), :
            ].astype(jnp.bfloat16)


def order_rows(blocks, rows, ordered):
    i, j = lax.axis_index("gy"), lax.axis_index("gx")
    for s, x in zip(FROM, blocks):
        rows[pl.ds(pl.multiple_of((j ^ s) * BLOCK, BLOCK), BLOCK), :] = x[...]
    count = SIDE * BLOCK
    r = lax.broadcasted_iota(jnp.int32, (count, count), 0)
    c = lax.broadcasted_iota(jnp.int32, (count, count), 1)
    place = r >> 4
    owner = i ^ (((place & 1) << 1) | (place >> 1))
    wanted = ((r & 12) << 2) | (owner << 2) | (r & 3)
    swap = jnp.where(c == wanted, 1.0, 0.0).astype(jnp.bfloat16)
    ordered[...] = jnp.dot(swap, rows[...], preferred_element_type=jnp.float32).astype(
        jnp.bfloat16
    )


def multiply(tile, ordered, w, keep, send):
    def step(n, _):
        at = pl.ds(pl.multiple_of(n * tile, tile), tile)
        acc = jnp.dot(ordered[...], w[:, at], preferred_element_type=jnp.float32)
        keep[:, at] = acc[: 2 * BLOCK]
        send[:, at] = acc[2 * BLOCK :]
        return 0

    lax.fori_loop(0, w.shape[1] // tile, step, 0)


def first_output_body(tile, x0, x1, x2, x3, w, ready, keep, send, ordered, rows):
    order_rows((x0, x1, x2, x3), rows, ordered)
    multiply(tile, ordered, w, keep, send)


def finish_body(keep0, got0, across0, keep1, got1, across1, out):
    first = keep0.shape[1]
    for keep, got, across, at in (
        (keep0, got0, across0, slice(0, first)),
        (keep1, got1, across1, slice(first, None)),
    ):
        total = (keep[:BLOCK, :] + got[:BLOCK, :]) + across[...].astype(jnp.float32)
        out[:, at] = total.astype(jnp.bfloat16)


def square_shards(
    tokens,
    w_query,
    key_matrix,
    value_matrix,
    w_output,
    stored_keys,
    stored_values,
    lengths,
    positions,
):
    f32, bf16 = jnp.float32, jnp.bfloat16
    depth, q_width = w_query.shape
    kv_width = key_matrix.shape[1]
    groups = kv_width // HEAD_WIDTH
    wide = groups * SLOTS

    angles = rotary_angles(positions)
    cosine, sine = jnp.cos(angles), jnp.sin(angles)
    cosine = jnp.concatenate([cosine, cosine], axis=1)
    sine = jnp.concatenate([-sine, sine], axis=1)

    near = partners(lambda k: tokens, "gx", TOKENS_FROM)
    tile = q_width // 2
    part = q_width // 2
    w_first, w_second, _ = fetch([(w_query, 0, part), (w_query, part, part)])
    sums = []
    for weights in ((w_first,), (w_second, key_matrix, value_matrix)):
        columns = sum(w.shape[1] for w in weights)
        half = jax.ShapeDtypeStruct((2, columns // HEAD_WIDTH * BLOCK, HEAD_WIDTH), f32)
        keep, send = call(
            functools.partial(project_body, tile, len(weights)),
            [half, half],
            (tokens, *near, *weights),
            [VMEM] * (4 + len(weights)),
            [pltpu.VMEM((SIDE * BLOCK, depth), bf16)],
            flops=2 * SIDE * BLOCK * depth * columns,
            moved=2 * depth * columns,
        )
        got = lax.ppermute(send, "gy", [(p, p ^ 1) for p in range(SIDE)])
        summed = keep[1] + got[1]
        sums += [keep, got, lax.ppermute(summed, "gy", [(p, p ^ 2) for p in range(SIDE)])]
    depth, out_width = w_output.shape
    part = out_width // 2
    stored_keys, stored_values, w_first, ready = fetch(
        [(stored_keys,), (stored_values,), (w_output, 0, part)], summed
    )
    piece = jax.ShapeDtypeStruct((ROWS * wide, HEAD_WIDTH), bf16)
    mine = call(
        functools.partial(spread_body, groups),
        [piece] * SIDE,
        (*sums, ready),
        [VMEM] * 7,
        [pltpu.VMEM((wide * BLOCK, HEAD_WIDTH), f32)],
    )
    others = partners(lambda k: mine[k], "gx", HEADS_FROM)
    context = call(
        functools.partial(attend_body, groups),
        [piece] * SIDE,
        (lengths, mine[0], *others, cosine, sine, stored_keys, stored_values),
        [SMEM] + [VMEM] * 8,
        [pltpu.VMEM((SIDE, ROWS * wide, HEAD_WIDTH), bf16)],
    )
    others = partners(lambda k: context[k], "gy", CONTEXT_FROM)
    rows = call(
        functools.partial(turn_body, groups),
        jax.ShapeDtypeStruct((BLOCK, groups * GROUP * HEAD_WIDTH), bf16),
        (context[0], *others),
        [VMEM] * 4,
        [pltpu.VMEM((SIDE * ROWS * wide, HEAD_WIDTH), f32)],
    )
    near = partners(lambda k: rows, "gx", FROM)
    w_second, ready = fetch([(w_output, part, part)], rows)
    sums = []
    for w in (w_first, w_second):
        columns = w.shape[1]
        half = jax.ShapeDtypeStruct((2 * BLOCK, columns), f32)
        flops, moved = 2 * SIDE * BLOCK * depth * columns, 2 * depth * columns
        if not sums:
            keep, send, ordered = call(
                functools.partial(first_output_body, tile),
                [half, half, jax.ShapeDtypeStruct((SIDE * BLOCK, depth), bf16)],
                (rows, *near, w, ready),
                [VMEM] * 6,
                [pltpu.VMEM((SIDE * BLOCK, depth), bf16)],
                flops=flops,
                moved=moved,
            )
        else:
            keep, send = call(
                functools.partial(multiply, tile),
                [half, half],
                (ordered, w),
                [VMEM] * 2,
                flops=flops,
                moved=moved,
            )
        got = lax.ppermute(send, "gy", [(p, p ^ 1) for p in range(SIDE)])
        summed = (keep[BLOCK:] + got[BLOCK:]).astype(bf16)
        sums += [keep, got, lax.ppermute(summed, "gy", [(p, p ^ 2) for p in range(SIDE)])]
    return call(
        finish_body, jax.ShapeDtypeStruct((BLOCK, out_width), bf16), sums, [VMEM] * 6
    )


def shards(*args):
    tokens, w_query, key_matrix, _, w_output, stored_keys, _, lengths, _ = args
    whole_heads = w_query.shape[1] % (GROUP * HEAD_WIDTH) == 0
    groups = key_matrix.shape[1] // HEAD_WIDTH
    square = (
        lax.axis_size("gx") == SIDE
        and lax.axis_size("gy") == SIDE
        and lengths.shape[0] == ROWS
        and tokens.shape[0] == BLOCK
        and whole_heads
        and groups * HEAD_WIDTH == key_matrix.shape[1]
        and groups * GROUP * HEAD_WIDTH == w_query.shape[1] == w_output.shape[0]
        and w_output.shape[1] == w_query.shape[1]
        and w_query.shape[1] % 1024 == 0
    )
    return square_shards(*args) if square else general_shards(*args)


def solution(mesh):
    in_specs = (
        P(("parts", "gx"), "gy"),
        P("gy", "gx"),
        P("gy", "gx"),
        P("gy", "gx"),
        P("gy", "gx"),
        P(("parts", "gy", "gx"), None, None),
        P(("parts", "gy", "gx"), None, None),
        P(("parts", "gy", "gx")),
        P(("parts", "gy", "gx")),
    )
    out_specs = P(("parts", "gy"), "gx")
    return jax.shard_map(shards, mesh=mesh, in_specs=in_specs, out_specs=out_specs, check_vma=False)
```

```python
import functools
import math

import jax
import jax.numpy as jnp
from jax import lax
from jax.experimental import pallas as pl
from jax.experimental.pallas import tpu as pltpu
from jax.sharding import PartitionSpec as P

QUERY_HEADS = 96
KEY_VALUE_HEADS = 8
HEAD_WIDTH = 128
CONTEXT_LENGTH = 128
GROUP = QUERY_HEADS // KEY_VALUE_HEADS


rope_theta = 1000000.0

VMEM = pl.BlockSpec(memory_space=pltpu.VMEM)
SMEM = pl.BlockSpec(memory_space=pltpu.SMEM)


def rotary_angles(positions):
    half_dim = HEAD_WIDTH // 2
    frequency = rope_theta ** (-(jnp.arange(half_dim, dtype=jnp.float32) * 2.0) / HEAD_WIDTH)
    return positions.astype(jnp.float32)[:, None] * frequency[None, :]


def rotary_table(values, positions, heads):
    number_rows = values.shape[0]
    head_size = values.shape[1] // heads
    half_dim = head_size // 2
    wide = values.astype(jnp.float32).reshape(number_rows, heads, head_size)
    angles = rotary_angles(positions)
    cosine = jnp.cos(angles)[:, None, :]
    sine = jnp.sin(angles)[:, None, :]
    lower_half = wide[..., :half_dim]
    upper_half = wide[..., half_dim:]
    turned = jnp.concatenate(
        [lower_half * cosine - upper_half * sine, upper_half * cosine + lower_half * sine], axis=-1
    )
    return turned.reshape(values.shape).astype(jnp.bfloat16)


def attend(rotated_query, rotated_key, fresh_value, device_keys, device_values, lengths):
    number_rows = rotated_query.shape[0]
    logit_scale = 1.0 / HEAD_WIDTH**0.5
    per_head_queries = rotated_query.reshape(number_rows, KEY_VALUE_HEADS, GROUP, HEAD_WIDTH)
    per_head_keys = device_keys.reshape(number_rows, CONTEXT_LENGTH, KEY_VALUE_HEADS, HEAD_WIDTH)
    scores = (
        jnp.einsum(
            "rgqd,rpgd->rgqp", per_head_queries, per_head_keys, preferred_element_type=jnp.float32
        )
        * logit_scale
    )
    live_mask = (jnp.arange(CONTEXT_LENGTH, dtype=jnp.int32)[None, :] < lengths[:, None])[
        :, None, None, :
    ]
    scores = jnp.where(live_mask, scores, -jnp.inf)
    self_score = (
        jnp.einsum(
            "uojn,uon->uoj",
            per_head_queries,
            rotated_key.reshape(number_rows, KEY_VALUE_HEADS, HEAD_WIDTH),
            preferred_element_type=jnp.float32,
        )
        * logit_scale
    )
    row_max = jnp.maximum(jnp.max(scores, axis=-1), self_score)
    cached_exp = jnp.exp(scores - row_max[..., None])
    own_exp = jnp.exp(self_score - row_max)
    totals = jnp.sum(cached_exp, axis=-1) + own_exp
    weights = (cached_exp / totals[..., None]).astype(jnp.bfloat16)
    self_weight = (own_exp / totals).astype(jnp.bfloat16)
    per_head_values = device_values.reshape(
        number_rows, CONTEXT_LENGTH, KEY_VALUE_HEADS, HEAD_WIDTH
    )
    context_window = jnp.einsum(
        "rgqp,rpgd->rgqd", weights, per_head_values, preferred_element_type=jnp.float32
    )
    context_window = context_window + self_weight.astype(jnp.float32)[
        ..., None
    ] * fresh_value.astype(jnp.float32).reshape(number_rows, KEY_VALUE_HEADS, 1, HEAD_WIDTH)
    return context_window.reshape(number_rows, QUERY_HEADS * HEAD_WIDTH).astype(jnp.bfloat16)


def general_shards(
    tokens,
    w_query,
    key_matrix,
    value_matrix,
    w_output,
    stored_keys,
    stored_values,
    lengths,
    positions,
):
    q_width = w_query.shape[1]
    kv_width = key_matrix.shape[1]
    piece = lax.all_gather(tokens, "gx", axis=0, tiled=True)
    partials = jnp.concatenate(
        [
            jnp.dot(piece, w_query, preferred_element_type=jnp.float32),
            jnp.dot(piece, key_matrix, preferred_element_type=jnp.float32),
            jnp.dot(piece, value_matrix, preferred_element_type=jnp.float32),
        ],
        axis=1,
    )
    summed = lax.psum_scatter(partials, "gy", scatter_dimension=0, tiled=True)
    query = summed[:, :q_width].astype(jnp.bfloat16)
    fresh_key = summed[:, q_width : q_width + kv_width].astype(jnp.bfloat16)
    fresh_value = summed[:, q_width + kv_width :].astype(jnp.bfloat16)
    query_rows, key_row_matrix, value_rows = (
        lax.all_to_all(query, "gx", split_axis=0, concat_axis=1, tiled=True),
        lax.all_to_all(fresh_key, "gx", split_axis=0, concat_axis=1, tiled=True),
        lax.all_to_all(fresh_value, "gx", split_axis=0, concat_axis=1, tiled=True),
    )
    rotated_query = rotary_table(query_rows, positions, QUERY_HEADS)
    rotated_key = rotary_table(key_row_matrix, positions, KEY_VALUE_HEADS)
    context_window = attend(
        rotated_query, rotated_key, value_rows, stored_keys, stored_values, lengths
    )
    out_width = w_output.shape[1]
    block_list = lax.all_to_all(context_window[None], "gy", split_axis=2, concat_axis=0, tiled=True)
    products = jnp.einsum(
        "jrd,de->jre",
        lax.all_gather(block_list, "gx", axis=1, tiled=True),
        w_output,
        preferred_element_type=jnp.float32,
    )
    products = products.reshape(-1, out_width)
    result = lax.psum_scatter(products, "gy", scatter_dimension=0, tiled=True)
    return result.astype(jnp.bfloat16)


SIDE = 4
ROWS = 4
BLOCK = SIDE * ROWS
SLOTS = 16
TOKENS_FROM = (0, 1, 2, 3)
FROM = (0, 3, 1, 2)
HEADS_FROM = (0, 2, 3, 1)
CONTEXT_FROM = (0, 2, 3, 1)


def call(body, outs, args, specs, scratch=(), limit=8, flops=0, moved=0):
    return pl.pallas_call(
        body,
        out_shape=outs,
        in_specs=specs,
        out_specs=jax.tree.map(lambda _: VMEM, outs),
        scratch_shapes=list(scratch),
        compiler_params=pltpu.CompilerParams(vmem_limit_bytes=limit << 20),
        cost_estimate=pl.CostEstimate(flops=flops, bytes_accessed=moved, transcendentals=0),
    )(*args)


def fetch_body(parts, *refs):
    sems, done = refs[-1], refs[-2]
    targets = refs[-2 - len(parts) : -2]
    copies = []
    for n, (source, index, pieces) in enumerate(parts):
        size = refs[source].shape[0] // pieces
        for k in range(pieces):
            at = pl.ds(k * size, size)
            copies.append(
                pltpu.make_async_copy(
                    refs[source].at[(at, *index)], targets[n].at[at], sems.at[len(copies)]
                )
            )
    for copy in copies:
        copy.start()
    done[...] = jnp.zeros_like(done)
    for copy in copies:
        copy.wait()


def fetch(parts, *after):
    sources, plan, outs = [], [], []
    for array, *columns in parts:
        if not any(array is s for s in sources):
            sources.append(array)
        at = next(n for n, s in enumerate(sources) if s is array)
        index = (slice(None), pl.ds(*columns)) if columns else ()
        shape = (array.shape[0], columns[1]) if columns else array.shape
        plan.append((at, index[1:], 4))
        outs.append(pltpu.VMEM(shape, array.dtype))
    moved = 2 * sum(math.prod(out.shape) for out in outs)
    done = jax.ShapeDtypeStruct((8, HEAD_WIDTH), jnp.float32)
    return pl.pallas_call(
        functools.partial(fetch_body, plan),
        out_shape=[*outs, done],
        in_specs=[pl.BlockSpec(memory_space=pltpu.HBM)] * len(sources) + [VMEM] * len(after),
        out_specs=[VMEM] * (len(outs) + 1),
        scratch_shapes=[pltpu.SemaphoreType.DMA((4 * len(outs),))],
        compiler_params=pltpu.CompilerParams(vmem_limit_bytes=36 << 20),
        cost_estimate=pl.CostEstimate(flops=0, bytes_accessed=moved, transcendentals=0),
    )(*sources, *after)


def partners(block, axis, order):
    return [lax.ppermute(block(k), axis, [(p, p ^ k) for p in range(SIDE)]) for k in order[1:]]


def project_body(tile, count, x0, x1, x2, x3, *refs):
    weights = refs[:count]
    keep, send, rows = refs[count:]
    m = lax.axis_index("gx") ^ lax.axis_index("gy")
    for s, x in zip(TOKENS_FROM, (x0, x1, x2, x3)):
        d = s ^ m
        place = ((d & 1) << 1) | (d >> 1)
        rows[pl.ds(pl.multiple_of(place * BLOCK, BLOCK), BLOCK), :] = x[...]

    def put(w, c, width, head):
        acc = jnp.dot(rows[...], w[:, pl.ds(c, width)], preferred_element_type=jnp.float32)
        for k in range(width // HEAD_WIDTH):
            at = pl.ds(pl.multiple_of((head + k) * BLOCK, BLOCK), BLOCK)
            part = acc[:, k * HEAD_WIDTH : (k + 1) * HEAD_WIDTH]
            for b in range(2):
                keep[b, at, :] = part[b * BLOCK : (b + 1) * BLOCK]
                send[b, at, :] = part[(2 + b) * BLOCK : (3 + b) * BLOCK]

    head = 0
    for w in weights:
        width = min(tile, w.shape[1])
        per = width // HEAD_WIDTH

        def step(n, _):
            put(w, pl.multiple_of(n * width, width), width, head + n * per)
            return 0

        lax.fori_loop(0, w.shape[1] // width, step, 0)
        head += w.shape[1] // HEAD_WIDTH


def spread_body(groups, keep0, got0, across0, keep1, got1, across1, ready, *refs):
    outs, slots = refs[:-1], refs[-1]
    j = lax.axis_index("gx")
    first = keep0.shape[1] // BLOCK
    qh = groups * GROUP
    for g in range(groups):
        for u in range(SLOTS):
            if u < GROUP:
                h = g * GROUP + u
            elif u == GROUP:
                h = qh + g
            elif u == GROUP + 1:
                h = qh + groups + g
            else:
                h = None
            at = (g * SLOTS + u) * BLOCK
            if h is None:
                slots[at : at + BLOCK, :] = jnp.zeros((BLOCK, HEAD_WIDTH), jnp.float32)
                continue
            keep, got, across = (keep0, got0, across0) if h < first else (keep1, got1, across1)
            h = h if h < first else h - first
            src = slice(h * BLOCK, (h + 1) * BLOCK)
            total = (keep[0, src, :] + got[0, src, :]) + across[src, :]
            slots[at : at + BLOCK, :] = total.astype(jnp.bfloat16).astype(jnp.float32)
    wide = groups * SLOTS
    for e, out in enumerate(outs):
        for t in range(ROWS):
            row = (j ^ e) * ROWS + t
            out[t * wide : (t + 1) * wide, :] = slots[pl.ds(row, wide, stride=BLOCK), :].astype(
                jnp.bfloat16
            )


def attend_body(
    groups, lengths, a0, a1, a2, a3, cosine, sine, keys, values, c0, c1, c2, c3, held
):
    j = lax.axis_index("gx")
    m = j ^ lax.axis_index("gy")
    scale = 1.0 / HEAD_WIDTH**0.5
    wide = groups * SLOTS
    span = groups * HEAD_WIDTH
    slot = lax.broadcasted_iota(jnp.int32, (wide, HEAD_WIDTH), 0)
    is_value = slot % SLOTS == GROUP + 1
    of_group = [slot // SLOTS == g for g in range(groups)]
    spot = lax.broadcasted_iota(jnp.int32, (wide, CONTEXT_LENGTH), 1)
    pieces = [(e, t) for e in range(SIDE) for t in range(ROWS)]
    heads = dict(zip(HEADS_FROM, (a0, a1, a2, a3)))

    def lanes(e):
        return pl.ds(pl.multiple_of((j ^ e) * span, span), span)

    def each_group(block, row):
        out = block[row : row + 1]
        for g in range(1, groups):
            at = g * SLOTS + row
            out = jnp.where(of_group[g], block[at : at + 1], out)
        return out

    scores, owns, fresh = [], [], []
    for e, t in pieces:
        raw = heads[e][t * wide : (t + 1) * wide, :].astype(jnp.float32)
        turned = (
            raw * cosine[t : t + 1, :] + pltpu.roll(raw, HEAD_WIDTH // 2, 1) * sine[t : t + 1, :]
        )
        q = jnp.where(is_value, raw, turned).astype(jnp.bfloat16)
        wide_q = q.astype(jnp.float32)
        spread = jnp.concatenate(
            [jnp.where(of_group[g], wide_q, 0.0) for g in range(groups)], axis=1
        ).astype(jnp.bfloat16)
        found = lax.dot_general(
            spread,
            keys[t, :, lanes(e)],
            (((1,), (1,)), ((), ())),
            preferred_element_type=jnp.float32,
        )
        scores.append(jnp.where(spot < lengths[t], found * scale, -jnp.inf))
        owns.append(
            jnp.sum(wide_q * each_group(wide_q, GROUP), axis=1, keepdims=True) * scale
        )
        fresh.append(each_group(wide_q, GROUP + 1))
    tops = [
        jnp.maximum(jnp.max(s, axis=1, keepdims=True), own) for s, own in zip(scores, owns)
    ]
    cached = [jnp.exp(s - top) for s, top in zip(scores, tops)]
    owns = [jnp.exp(own - top) for own, top in zip(owns, tops)]
    totals = [jnp.sum(w, axis=1, keepdims=True) + own for w, own in zip(cached, owns)]
    weights = [(w / total).astype(jnp.bfloat16) for w, total in zip(cached, totals)]
    owns = [
        (own / total).astype(jnp.bfloat16).astype(jnp.float32) for own, total in zip(owns, totals)
    ]
    for n, (e, t) in enumerate(pieces):
        found = jnp.dot(weights[n], values[t, :, lanes(e)], preferred_element_type=jnp.float32)
        context = found[:, :HEAD_WIDTH]
        for g in range(1, groups):
            context = jnp.where(
                of_group[g], found[:, g * HEAD_WIDTH : (g + 1) * HEAD_WIDTH], context
            )
        context = context + owns[n] * fresh[n]
        held[e ^ m, t * wide : (t + 1) * wide, :] = context.astype(jnp.bfloat16)
    for f, c in enumerate((c0, c1, c2, c3)):
        c[...] = held[f]


def turn_body(groups, c0, c1, c2, c3, out, slots):
    i = lax.axis_index("gy")
    wide = groups * SLOTS
    size = ROWS * wide
    for f, c in zip(CONTEXT_FROM, (c0, c1, c2, c3)):
        slots[pl.ds(pl.multiple_of((i ^ f) * size, size), size), :] = c[...].astype(jnp.float32)
    for g in range(groups):
        for u in range(GROUP):
            h = g * GROUP + u
            out[:, h * HEAD_WIDTH : (h + 1) * HEAD_WIDTH] = slots[
                pl.ds(g * SLOTS + u, BLOCK, stride=wide), :
            ].astype(jnp.bfloat16)


def order_rows(blocks, rows, ordered):
    i, j = lax.axis_index("gy"), lax.axis_index("gx")
    for s, x in zip(FROM, blocks):
        rows[pl.ds(pl.multiple_of((j ^ s) * BLOCK, BLOCK), BLOCK), :] = x[...]
    count = SIDE * BLOCK
    r = lax.broadcasted_iota(jnp.int32, (count, count), 0)
    c = lax.broadcasted_iota(jnp.int32, (count, count), 1)
    place = r >> 4
    owner = i ^ (((place & 1) << 1) | (place >> 1))
    wanted = ((r & 12) << 2) | (owner << 2) | (r & 3)
    swap = jnp.where(c == wanted, 1.0, 0.0).astype(jnp.bfloat16)
    ordered[...] = jnp.dot(swap, rows[...], preferred_element_type=jnp.float32).astype(
        jnp.bfloat16
    )


def multiply(tile, ordered, w, keep, send):
    def step(n, _):
        at = pl.ds(pl.multiple_of(n * tile, tile), tile)
        acc = jnp.dot(ordered[...], w[:, at], preferred_element_type=jnp.float32)
        keep[:, at] = acc[: 2 * BLOCK]
        send[:, at] = acc[2 * BLOCK :]
        return 0

    lax.fori_loop(0, w.shape[1] // tile, step, 0)


def first_output_body(tile, x0, x1, x2, x3, w, ready, keep, send, ordered, rows):
    order_rows((x0, x1, x2, x3), rows, ordered)
    multiply(tile, ordered, w, keep, send)


def finish_body(keep0, got0, across0, keep1, got1, across1, out):
    first = keep0.shape[1]
    for keep, got, across, at in (
        (keep0, got0, across0, slice(0, first)),
        (keep1, got1, across1, slice(first, None)),
    ):
        total = (keep[:BLOCK, :] + got[:BLOCK, :]) + across[...].astype(jnp.float32)
        out[:, at] = total.astype(jnp.bfloat16)


def square_shards(
    tokens,
    w_query,
    key_matrix,
    value_matrix,
    w_output,
    stored_keys,
    stored_values,
    lengths,
    positions,
):
    f32, bf16 = jnp.float32, jnp.bfloat16
    depth, q_width = w_query.shape
    kv_width = key_matrix.shape[1]
    groups = kv_width // HEAD_WIDTH
    wide = groups * SLOTS

    angles = rotary_angles(positions)
    cosine, sine = jnp.cos(angles), jnp.sin(angles)
    cosine = jnp.concatenate([cosine, cosine], axis=1)
    sine = jnp.concatenate([-sine, sine], axis=1)

    near = partners(lambda k: tokens, "gx", TOKENS_FROM)
    tile = q_width // 2
    part = q_width // 2
    w_first, w_second, _ = fetch([(w_query, 0, part), (w_query, part, part)])
    sums = []
    for weights in ((w_first,), (w_second, key_matrix, value_matrix)):
        columns = sum(w.shape[1] for w in weights)
        half = jax.ShapeDtypeStruct((2, columns // HEAD_WIDTH * BLOCK, HEAD_WIDTH), f32)
        keep, send = call(
            functools.partial(project_body, tile, len(weights)),
            [half, half],
            (tokens, *near, *weights),
            [VMEM] * (4 + len(weights)),
            [pltpu.VMEM((SIDE * BLOCK, depth), bf16)],
            flops=2 * SIDE * BLOCK * depth * columns,
            moved=2 * depth * columns,
        )
        got = lax.ppermute(send, "gy", [(p, p ^ 1) for p in range(SIDE)])
        summed = keep[1] + got[1]
        sums += [keep, got, lax.ppermute(summed, "gy", [(p, p ^ 2) for p in range(SIDE)])]
    depth, out_width = w_output.shape
    part = out_width // 2
    w_first, ready = fetch([(w_output, 0, part)], summed)
    piece = jax.ShapeDtypeStruct((ROWS * wide, HEAD_WIDTH), bf16)
    mine = call(
        functools.partial(spread_body, groups),
        [piece] * SIDE,
        (*sums, ready),
        [VMEM] * 7,
        [pltpu.VMEM((wide * BLOCK, HEAD_WIDTH), f32)],
    )
    others = partners(lambda k: mine[k], "gx", HEADS_FROM)
    context = call(
        functools.partial(attend_body, groups),
        [piece] * SIDE,
        (lengths, mine[0], *others, cosine, sine, stored_keys, stored_values),
        [SMEM] + [VMEM] * 8,
        [pltpu.VMEM((SIDE, ROWS * wide, HEAD_WIDTH), bf16)],
    )
    others = partners(lambda k: context[k], "gy", CONTEXT_FROM)
    rows = call(
        functools.partial(turn_body, groups),
        jax.ShapeDtypeStruct((BLOCK, groups * GROUP * HEAD_WIDTH), bf16),
        (context[0], *others),
        [VMEM] * 4,
        [pltpu.VMEM((SIDE * ROWS * wide, HEAD_WIDTH), f32)],
    )
    near = partners(lambda k: rows, "gx", FROM)
    w_second, ready = fetch([(w_output, part, part)], rows)
    sums = []
    for w in (w_first, w_second):
        columns = w.shape[1]
        half = jax.ShapeDtypeStruct((2 * BLOCK, columns), f32)
        flops, moved = 2 * SIDE * BLOCK * depth * columns, 2 * depth * columns
        if not sums:
            keep, send, ordered = call(
                functools.partial(first_output_body, tile),
                [half, half, jax.ShapeDtypeStruct((SIDE * BLOCK, depth), bf16)],
                (rows, *near, w, ready),
                [VMEM] * 6,
                [pltpu.VMEM((SIDE * BLOCK, depth), bf16)],
                flops=flops,
                moved=moved,
            )
        else:
            keep, send = call(
                functools.partial(multiply, tile),
                [half, half],
                (ordered, w),
                [VMEM] * 2,
                flops=flops,
                moved=moved,
            )
        got = lax.ppermute(send, "gy", [(p, p ^ 1) for p in range(SIDE)])
        summed = (keep[BLOCK:] + got[BLOCK:]).astype(bf16)
        sums += [keep, got, lax.ppermute(summed, "gy", [(p, p ^ 2) for p in range(SIDE)])]
    return call(
        finish_body, jax.ShapeDtypeStruct((BLOCK, out_width), bf16), sums, [VMEM] * 6
    )


def shards(*args):
    tokens, w_query, key_matrix, _, w_output, stored_keys, _, lengths, _ = args
    whole_heads = w_query.shape[1] % (GROUP * HEAD_WIDTH) == 0
    groups = key_matrix.shape[1] // HEAD_WIDTH
    square = (
        lax.axis_size("gx") == SIDE
        and lax.axis_size("gy") == SIDE
        and lengths.shape[0] == ROWS
        and tokens.shape[0] == BLOCK
        and whole_heads
        and groups * HEAD_WIDTH == key_matrix.shape[1]
        and groups * GROUP * HEAD_WIDTH == w_query.shape[1] == w_output.shape[0]
        and w_output.shape[1] == w_query.shape[1]
        and w_query.shape[1] % 1024 == 0
    )
    return square_shards(*args) if square else general_shards(*args)


def solution(mesh):
    in_specs = (
        P(("parts", "gx"), "gy"),
        P("gy", "gx"),
        P("gy", "gx"),
        P("gy", "gx"),
        P("gy", "gx"),
        P(("parts", "gy", "gx"), None, None),
        P(("parts", "gy", "gx"), None, None),
        P(("parts", "gy", "gx")),
        P(("parts", "gy", "gx")),
    )
    out_specs = P(("parts", "gy"), "gx")
    return jax.shard_map(shards, mesh=mesh, in_specs=in_specs, out_specs=out_specs, check_vma=False)
```
